512 devices in a mesh: row: 32 (over x_lo, z, core), blk: 16 (over x_hi, y).
Axes of the slice: x: 4 (x_hi: 2, x_lo: 2; x = x_hi * 2 + x_lo), y: 8, z: 8, core: 2. Of those that a mesh axis runs over, the one named last changes fastest.
Arguments:
- queries: bfloat16 [128, 2048, 128], P('row', 'blk'), may hold values from -6 to 6
- keys: bfloat16 [128, 2048, 128], P('row', 'blk'), may hold values from -6 to 6
- values: bfloat16 [128, 2048, 128], P('row', 'blk'), may hold values from -6 to 6
- bias: bfloat16 [4, 2048, 2048], P(None, 'blk'), may hold values from -6 to 6
- out_grad: bfloat16 [128, 2048, 128], P('row', 'blk'), may hold values from -48 to 48
- outputs: bfloat16 [128, 2048, 128], P('row', 'blk'), may hold values from -1.5 to 1.5
- logsumexp: float32 [128, 4, 2048], P('row', None, 'blk'), may hold values from 8 to 9.5
Outputs:
- query_grad: bfloat16 [128, 2048, 128], P('row', 'blk')
- key_grad: bfloat16 [128, 2048, 128], P('row', 'blk')
- value_grad: bfloat16 [128, 2048, 128], P('row', 'blk')
- bias_grad: float32 [4, 2048, 2048], P(None, 'blk', 'row')
The draws below stay inside these ranges and needn't reach their ends.
All inputs are finite; a program needn't handle non-finite values.
Results may differ from the reference program's by a relative error of at most 0.0049.
Values may be sent and summed in bfloat16 or wider, within the bound.
No kernel may reach another device: no remote copies, remote signals or barrier semaphores. Data moves between devices by JAX's collectives and lax.ppermute only.
A program may use at most 64 MiB of HBM per device.

```python
import jax
import jax.numpy as jnp
from jax import lax

HEADS = 4
WIDTH = 128
ROWS = 128
NODES = 2048


def level_of(stream_key, shape, split, smallest, top_value):
    def one(axis_at, shards_of):
        draws = jax.random.uniform(jax.random.fold_in(jax.random.fold_in(stream_key, 6), axis_at), (shards_of,), jnp.float32, smallest / len(split), top_value / len(split))
        return jnp.repeat(jnp.exp(draws), shape[axis_at] // shards_of).reshape((-1,) + (1,) * (len(shape) - axis_at - 1))

    gain = one(*split[0])
    for cut in split[1:]:
        gain = gain * one(*cut)
    return gain


def bell_draw(own_key, dims, scale, limit, cuts=(), kind=jnp.bfloat16):
    entries = scale * jax.random.normal(own_key, dims, jnp.float32)
    if cuts:
        entries = entries * level_of(own_key, dims, cuts, -0.22, 0.18)
    return jnp.clip(entries, -limit, limit).astype(kind)


def setup_inputs(seed: int = 0) -> dict:
    seeds = jax.random.split(jax.random.key(seed), 8)
    return {
        "queries": bell_draw(seeds[0], (ROWS, NODES, WIDTH), 1.0, 6.0, ((0, 32), (1, 16))),
        "keys": bell_draw(seeds[1], (ROWS, NODES, WIDTH), 1.0, 6.0, ((0, 32), (1, 16))),
        "values": bell_draw(seeds[2], (ROWS, NODES, WIDTH), 1.0, 6.0, ((0, 32), (1, 16))),
        "bias": bell_draw(seeds[3], (HEADS, NODES, NODES), 1.0, 6.0, ((1, 16),)),
        "out_grad": bell_draw(seeds[4], (ROWS, NODES, WIDTH), 8.0, 48.0, ((0, 32), (1, 16))),
        "outputs": bell_draw(seeds[5], (ROWS, NODES, WIDTH), 0.25, 1.5, ((0, 32), (1, 16))),
        "logsumexp": jnp.clip(8.0 + 1.5 * jax.random.uniform(seeds[6], (ROWS, HEADS, NODES), jnp.float32) ** level_of(seeds[6], (ROWS, HEADS, NODES), ((0, 32), (2, 16)), -0.2, 0.2), 8.0, 9.5),
    }


def reference(queries, keys, values, bias, out_grad, outputs, logsumexp):
    rows, nodes, width = queries.shape
    heads = bias.shape[0]
    head_dim = width // heads
    scale = head_dim ** -0.5
    bias_wide = bias.astype(jnp.float32)

    def one_row(carry, item):
        query_row, key_row, value_row, grad_row, output_row, offset = item
        query_f = query_row.astype(jnp.float32).reshape(nodes, heads, head_dim)
        key_f = key_row.astype(jnp.float32).reshape(nodes, heads, head_dim)
        value_f = value_row.astype(jnp.float32).reshape(nodes, heads, head_dim)
        grad_f = grad_row.astype(jnp.float32).reshape(nodes, heads, head_dim)
        output_f = output_row.astype(jnp.float32).reshape(nodes, heads, head_dim)
        delta = jnp.sum(grad_f * output_f, axis=-1).T
        scores = jnp.einsum('jhd,khd->hjk', query_f, key_f) * scale + bias_wide
        probs = jnp.exp(scores - offset[:, :, None])
        probs_low = lax.optimization_barrier(probs.astype(jnp.bfloat16)).astype(jnp.float32)
        value_grad = jnp.einsum('hjk,jhd->khd', probs_low, grad_f)
        prob_grad = jnp.einsum('jhd,khd->hjk', grad_f, value_f)
        score_grad = probs * (prob_grad - delta[:, :, None])
        score_low = lax.optimization_barrier(score_grad.astype(jnp.bfloat16)).astype(jnp.float32)
        query_grad = jnp.einsum('hjk,khd->jhd', score_low, key_f) * scale
        key_grad = jnp.einsum('hjk,jhd->khd', score_low, query_f) * scale
        outs = (query_grad.reshape(nodes, width).astype(jnp.bfloat16),
                key_grad.reshape(nodes, width).astype(jnp.bfloat16),
                value_grad.reshape(nodes, width).astype(jnp.bfloat16))
        return carry + score_grad, outs

    start = jnp.zeros((heads, nodes, nodes), jnp.float32)
    bias_grad, (query_grad, key_grad, value_grad) = lax.scan(
        one_row, start, (queries, keys, values, out_grad, outputs, logsumexp))
    return query_grad, key_grad, value_grad, bias_grad
```

```python
import functools

import jax
import jax.numpy as jnp
from jax import lax
from jax.experimental import pallas as pl
from jax.experimental.pallas import tpu as pltpu
from jax.sharding import Mesh
from jax.sharding import PartitionSpec as P

ROW = ("xl", "z", "c")
BLK = ("xh", "yh", "yl")
QUERY_GROUP = ("xl", "c", "xh", "yl")
KEY_GROUP = ("xl", "c", "yh")
LOG2E = 1.4426950408889634
AUG = 16
F32, BF16 = jnp.float32, jnp.bfloat16


def three_parts(x):
    high = x.astype(BF16).astype(F32)
    rest = x - high
    mid = rest.astype(BF16).astype(F32)
    return high, mid, rest - mid


def pack_kernel(scale, which_ref, q_ref, k_ref, v_ref, g_ref, o_ref, l_ref, bias_ref, to_query_ref, to_key_ref):
    quarter = pl.multiple_of(which_ref[0] * 32, 32)
    lines = lax.broadcasted_iota(jnp.int32, (AUG, 128), 0)
    for i in range(4):
        k_t = k_ref[i].astype(F32).T.astype(BF16)
        v_t = v_ref[i].astype(F32).T.astype(BF16)
        q_t = q_ref[i].astype(F32).T.astype(BF16)
        g_f = g_ref[i].astype(F32)
        g_t = g_f.T
        gg = (g_f * o_ref[i].astype(F32)).T
        g_t = g_t.astype(BF16)
        for h in range(4):
            part = slice(h * 32, h * 32 + 32)
            offset = l_ref[i, h : h + 1, :] * (-1.0 / scale)
            delta = -jnp.sum(gg[part], axis=0, keepdims=True)
            extra = jnp.zeros((AUG, 128), F32)
            for at, piece in enumerate(three_parts(offset) + three_parts(delta)):
                extra = jnp.where(lines == at, piece, extra)
            extra = extra.astype(BF16)
            for a in range(4):
                to_query_ref[h * 4 + a, i * 80 : i * 80 + 32, :] = q_t[part]
                to_query_ref[h * 4 + a, i * 80 + 32 : i * 80 + 48, :] = extra
                to_query_ref[h * 4 + a, i * 80 + 48 : i * 80 + 80, :] = g_t[part]
                to_key_ref[h * 4 + a, i * 64 : i * 64 + 32, :] = k_t[part]
                to_key_ref[h * 4 + a, i * 64 + 32 : i * 64 + 64, :] = v_t[part]
    for h in range(4):
        for a in range(4):
            for yh in range(4):
                block = (a // 2) * 8 + yh * 2 + a % 2
                to_query_ref[h * 4 + a, 320 + yh * 32 : 352 + yh * 32, :] = bias_ref[
                    h, pl.ds(quarter, 32), block * 128 : block * 128 + 128
                ]


def attend_kernel(scale, chunk, jq_ref, kv_ref, dq_ref, dkv_ref, db_ref, bias_s, acc_s):
    for a in range(4):
        for s in range(4):
            for yh in range(4):
                bias_s[a * 128 + s * 32 : a * 128 + s * 32 + 32, yh * 128 : yh * 128 + 128] = (
                    jq_ref[s * 4 + a, 320 + yh * 32 : 352 + yh * 32, :].astype(F32) * LOG2E
                )
    acc_s[...] = jnp.zeros_like(acc_s)
    lines = lax.broadcasted_iota(jnp.int32, (AUG, 512), 0)
    ones_offset = jnp.where(lines < 3, 1.0, 0.0).astype(BF16)
    ones_delta = jnp.where((lines >= 3) & (lines < 6), 1.0, 0.0).astype(BF16)
    dims = (((0,), (0,)), ((), ()))

    def one_row(t, carry):
        s, i = t // 4, t % 4
        base = s * 4
        jb = pl.multiple_of(i * 80, 16)
        kb = pl.multiple_of(i * 64, 16)
        whole = jnp.concatenate([jq_ref[base + a, pl.ds(jb, 80), :] for a in range(4)], axis=1)
        keys = jnp.concatenate([kv_ref[base + b, pl.ds(kb, 64), :] for b in range(4)], axis=1)
        k_t, v_t = keys[:32], keys[32:]
        k_aug = jnp.concatenate([k_t, ones_offset], axis=0)
        v_aug = jnp.concatenate([ones_delta, v_t], axis=0)
        dk = dv = None
        for n in range(512 // chunk):
            at = slice(n * chunk, n * chunk + chunk)
            q_aug = whole[:48, at]
            g_aug = whole[32:80, at]
            scores = lax.dot_general(q_aug, k_aug, dims, preferred_element_type=F32)
            probs = jnp.exp2(scores * (scale * LOG2E) + bias_s[at, :])
            prob_grad = lax.dot_general(g_aug, v_aug, dims, preferred_element_type=F32)
            score_grad = probs * prob_grad
            acc_s[at, :] += score_grad
            low = score_grad.astype(BF16)
            dv_n = jnp.dot(whole[48:80, at], probs.astype(BF16), preferred_element_type=F32)
            dk_n = jnp.dot(whole[:32, at], low, preferred_element_type=F32)
            dv = dv_n if dv is None else dv + dv_n
            dk = dk_n if dk is None else dk + dk_n
            dq = lax.dot_general(k_t, low, (((1,), (1,)), ((), ())), preferred_element_type=F32)
            dq = (dq * scale).astype(BF16)
            for m in range(chunk // 128):
                dq_ref[base + n * (chunk // 128) + m, pl.ds(pl.multiple_of(i * 32, 32), 32), :] = dq[
                    :, m * 128 : m * 128 + 128
                ]
        dk = (dk * scale).astype(BF16)
        dv = dv.astype(BF16)
        for b in range(4):
            dkv_ref[base + b, pl.ds(kb, 32), :] = dk[:, b * 128 : b * 128 + 128]
            dkv_ref[base + b, pl.ds(pl.multiple_of(kb + 32, 16), 32), :] = dv[:, b * 128 : b * 128 + 128]
        return carry

    lax.fori_loop(0, 16, one_row, 0)
    for yh in range(4):
        for half in range(2):
            db_ref[yh * 2 + half] = acc_s[half * 256 : half * 256 + 256, yh * 128 : yh * 128 + 128].astype(BF16)


def unpack_kernel(q_ref, kv_ref, dq_ref, dk_ref, dv_ref):
    for i in range(4):
        for ref, width, first, out in ((q_ref, 32, 0, dq_ref), (kv_ref, 64, 0, dk_ref), (kv_ref, 64, 32, dv_ref)):
            at = slice(i * width + first, i * width + first + 32)
            heads = []
            for h in range(4):
                total = ref[h * 4, at, :].astype(F32)
                for a in range(1, 4):
                    total = total + ref[h * 4 + a, at, :].astype(F32)
                heads.append(total)
            out[i] = jnp.concatenate(heads, axis=0).T.astype(BF16)


def vmem(n=1):
    return [pl.BlockSpec(memory_space=pltpu.VMEM)] * n


def params():
    return pltpu.CompilerParams(vmem_limit_bytes=40 * 2**20)


def bias_moves():
    pairs = []
    for xl in range(2):
        for z in range(8):
            for c in range(2):
                for xh in range(2):
                    for yl in range(2):
                        source = (((xl * 8 + z) * 2 + c) * 2 + xh) * 2 + yl
                        target = (((xh * 8 + (z // 2) * 2 + yl) * 2 + xl) * 2 + z % 2) * 2 + c
                        pairs.append((source, target))
    return pairs


def body(queries, keys, values, bias, out_grad, outputs, logsumexp):
    scale = 32 ** (-0.5)
    shape = lambda *s: jax.ShapeDtypeStruct(s, BF16)
    which = (lax.axis_index("xl") * 2 + lax.axis_index("c")).astype(jnp.int32).reshape(1)
    to_query, to_key = pl.pallas_call(
        functools.partial(pack_kernel, scale),
        out_shape=(shape(16, 448, 128), shape(16, 256, 128)),
        in_specs=[pl.BlockSpec(memory_space=pltpu.SMEM)] + vmem(7),
        out_specs=tuple(vmem(2)),
        compiler_params=params(),
        name="pack",
    )(which, queries, keys, values, out_grad, outputs, logsumexp, bias)
    got_key = lax.all_to_all(to_key, KEY_GROUP, 0, 0)
    got_query = lax.all_to_all(to_query, QUERY_GROUP, 0, 0)
    dq_parts, dkv_parts, db_parts = pl.pallas_call(
        functools.partial(attend_kernel, scale, 256),
        out_shape=(shape(16, 128, 128), shape(16, 256, 128), shape(8, 256, 128)),
        in_specs=vmem(2),
        out_specs=tuple(vmem(3)),
        scratch_shapes=[pltpu.VMEM((512, 512), F32), pltpu.VMEM((512, 512), F32)],
        compiler_params=params(),
        name="attend",
    )(got_query, got_key)
    db = lax.all_to_all(db_parts, "z", 0, 0)
    db = jnp.sum(db.astype(F32), axis=0)
    db = lax.ppermute(db, ROW + ("xh", "yl"), bias_moves())
    db = db.reshape(2, 128, 2, 64).transpose(2, 0, 1, 3).reshape(4, 128, 64)
    bias_grad = lax.all_to_all(db, ("c", "yl"), 0, 0)
    dkv = lax.all_to_all(dkv_parts, KEY_GROUP, 0, 0)
    dq = lax.all_to_all(dq_parts, QUERY_GROUP, 0, 0)
    query_grad, key_grad, value_grad = pl.pallas_call(
        unpack_kernel,
        out_shape=(shape(4, 128, 128),) * 3,
        in_specs=vmem(2),
        out_specs=tuple(vmem(3)),
        compiler_params=params(),
        name="unpack",
    )(dq, dkv)
    return query_grad, key_grad, value_grad, bias_grad


def solution(mesh):
    fine = Mesh(mesh.devices.reshape(2, 8, 2, 2, 4, 2), ROW + BLK)
    rows = P(ROW, BLK, None)
    in_specs = (rows, rows, rows, P(None, BLK, None), rows, rows, P(ROW, None, BLK))
    out_specs = (rows, rows, rows, P(None, BLK, ROW))
    return jax.shard_map(body, mesh=fine, in_specs=in_specs, out_specs=out_specs, check_vma=False)
```

```python
import functools

import jax
import jax.numpy as jnp
from jax import lax
from jax.experimental import pallas as pl
from jax.experimental.pallas import tpu as pltpu
from jax.sharding import Mesh
from jax.sharding import PartitionSpec as P

ROW = ("xl", "z", "c")
BLK = ("xh", "yh", "yl")
QUERY_GROUP = ("xl", "c", "xh", "yl")
KEY_GROUP = ("xl", "c", "yh")
LOG2E = 1.4426950408889634
AUG = 16
F32, BF16 = jnp.float32, jnp.bfloat16


def three_parts(x):
    high = x.astype(BF16).astype(F32)
    rest = x - high
    mid = rest.astype(BF16).astype(F32)
    return high, mid, rest - mid


def fetch(pairs, sems):
    copies = [pltpu.make_async_copy(src, dst, sems.at[at]) for at, (src, dst) in enumerate(pairs)]
    for copy in copies:
        copy.start()
    return copies


def turned(x):
    return x.astype(F32).T.astype(BF16)


def pack_key_kernel(k_hbm, v_hbm, to_key_ref, k_ref, v_ref, sems):
    copies = fetch(((k_hbm, k_ref), (v_hbm, v_ref)), sems)
    for copy in copies:
        copy.wait()
    for i in range(4):
        k_t, v_t = turned(k_ref[i]), turned(v_ref[i])
        for h in range(4):
            part = slice(h * 32, h * 32 + 32)
            for b in range(4):
                to_key_ref[h * 4 + b, i * 64 : i * 64 + 32, :] = k_t[part]
                to_key_ref[h * 4 + b, i * 64 + 32 : i * 64 + 64, :] = v_t[part]


def pack_query_kernel(
    scale, which_ref, q_hbm, g_hbm, o_hbm, l_hbm, bias_hbm, to_query_ref, q_ref, g_ref, o_ref, l_ref, bias_ref, sems
):
    quarter = pl.multiple_of(which_ref[0] * 32, 32)
    copies = fetch(
        (
            (q_hbm, q_ref),
            (g_hbm, g_ref),
            (o_hbm, o_ref),
            (l_hbm, l_ref),
            (bias_hbm.at[:, pl.ds(quarter, 32), :], bias_ref),
        ),
        sems,
    )
    lines = lax.broadcasted_iota(jnp.int32, (AUG, 128), 0)
    for copy in copies[:4]:
        copy.wait()
    for pair in range(2):
        extra = [jnp.zeros((AUG, 128), F32)] * 4
        for n in range(2):
            i = pair * 2 + n
            q_t = turned(q_ref[i])
            g_f = g_ref[i].astype(F32)
            gg = (g_f * o_ref[i].astype(F32)).T
            g_t = g_f.T.astype(BF16)
            for h in range(4):
                part = slice(h * 32, h * 32 + 32)
                offset = l_ref[i, h : h + 1, :] * (-1.0 / scale)
                delta = -jnp.sum(gg[part], axis=0, keepdims=True)
                for at, piece in enumerate(three_parts(offset) + three_parts(delta)):
                    extra[h] = jnp.where(lines == n * 6 + at, piece, extra[h])
                for a in range(4):
                    to_query_ref[h * 4 + a, i * 64 : i * 64 + 32, :] = q_t[part]
                    to_query_ref[h * 4 + a, i * 64 + 32 : i * 64 + 64, :] = g_t[part]
        for h in range(4):
            for a in range(4):
                to_query_ref[h * 4 + a, 256 + pair * 16 : 272 + pair * 16, :] = extra[h].astype(BF16)
    copies[4].wait()
    for h in range(4):
        for a in range(4):
            for yh in range(4):
                block = (a // 2) * 8 + yh * 2 + a % 2
                to_query_ref[h * 4 + a, 288 + yh * 32 : 320 + yh * 32, :] = bias_ref[
                    h, :, block * 128 : block * 128 + 128
                ]


def attend_kernel(scale, jq_ref, kv_ref, dq_ref, dkv_ref, db_ref, bias_s, acc_s):
    for a in range(4):
        for s in range(4):
            for yh in range(4):
                bias_s[a * 128 + s * 32 : a * 128 + s * 32 + 32, yh * 128 : yh * 128 + 128] = (
                    jq_ref[s * 4 + a, 288 + yh * 32 : 320 + yh * 32, :].astype(F32) * LOG2E
                )
    acc_s[...] = jnp.zeros_like(acc_s)
    lines = lax.broadcasted_iota(jnp.int32, (AUG, 512), 0)
    ones = [
        jnp.where((lines >= first) & (lines < first + 3), 1.0, 0.0).astype(BF16) for first in (0, 3, 6, 9)
    ]

    def four_rows(s, carry):
        base = s * 4
        for i in range(4):
            first = i * 64
            at = 256 + (i // 2) * 16
            q_t, g_t, extra = (
                jnp.concatenate([jq_ref[base + a, start : start + size, :] for a in range(4)], axis=1)
                for start, size in ((first, 32), (first + 32, 32), (at, 16))
            )
            k_t, v_t = (
                jnp.concatenate([kv_ref[base + b, start : start + 32, :] for b in range(4)], axis=1)
                for start in (first, first + 32)
            )
            q_rows = jnp.concatenate([q_t, extra], axis=0).T
            g_rows = jnp.concatenate([g_t, extra], axis=0).T
            k_aug = jnp.concatenate([k_t, ones[(i % 2) * 2]], axis=0)
            v_aug = jnp.concatenate([v_t, ones[(i % 2) * 2 + 1]], axis=0)
            scores = jnp.dot(q_rows, k_aug, preferred_element_type=F32)
            prob_grad = jnp.dot(g_rows, v_aug, preferred_element_type=F32)
            probs = jnp.exp2(scores * (scale * LOG2E) + bias_s[...])
            score_grad = probs * prob_grad
            acc_s[...] += score_grad
            low = score_grad.astype(BF16)
            dv = jnp.dot(g_t, probs.astype(BF16), preferred_element_type=F32).astype(BF16)
            dk = (jnp.dot(q_t, low, preferred_element_type=F32) * scale).astype(BF16)
            dq = (jnp.dot(low, k_t.T, preferred_element_type=F32).T * scale).astype(BF16)
            for b in range(4):
                block = slice(b * 128, b * 128 + 128)
                dq_ref[base + b, i * 32 : i * 32 + 32, :] = dq[:, block]
                dkv_ref[base + b, first : first + 32, :] = dk[:, block]
                dkv_ref[base + b, first + 32 : first + 64, :] = dv[:, block]
        return carry

    lax.fori_loop(0, 4, four_rows, 0)
    for yh in range(4):
        for half in range(2):
            db_ref[yh * 2 + half] = acc_s[half * 256 : half * 256 + 256, yh * 128 : yh * 128 + 128].astype(BF16)


def unpack_kernel(q_ref, kv_ref, dq_ref, dk_ref, dv_ref):
    for i in range(4):
        for ref, width, first, out in ((q_ref, 32, 0, dq_ref), (kv_ref, 64, 0, dk_ref), (kv_ref, 64, 32, dv_ref)):
            at = slice(i * width + first, i * width + first + 32)
            heads = []
            for h in range(4):
                total = ref[h * 4, at, :].astype(F32)
                for a in range(1, 4):
                    total = total + ref[h * 4 + a, at, :].astype(F32)
                heads.append(total)
            out[i] = jnp.concatenate(heads, axis=0).T.astype(BF16)


def vmem(n=1):
    return [pl.BlockSpec(memory_space=pltpu.VMEM)] * n


def params(mib=40):
    return pltpu.CompilerParams(vmem_limit_bytes=mib * 2**20)


def bias_moves():
    pairs = []
    for xl in range(2):
        for z in range(8):
            for c in range(2):
                for xh in range(2):
                    for yl in range(2):
                        source = (((xl * 8 + z) * 2 + c) * 2 + xh) * 2 + yl
                        target = (((xh * 8 + (z // 2) * 2 + yl) * 2 + xl) * 2 + z % 2) * 2 + c
                        pairs.append((source, target))
    return pairs


def body(queries, keys, values, bias, out_grad, outputs, logsumexp):
    scale = 32 ** (-0.5)
    shape = lambda *s: jax.ShapeDtypeStruct(s, BF16)
    which = (lax.axis_index("xl") * 2 + lax.axis_index("c")).astype(jnp.int32).reshape(1)
    hbm = pl.BlockSpec(memory_space=pltpu.HBM)
    to_key = pl.pallas_call(
        pack_key_kernel,
        out_shape=shape(16, 256, 128),
        in_specs=[hbm] * 2,
        out_specs=vmem()[0],
        scratch_shapes=[pltpu.VMEM((4, 128, 128), BF16)] * 2 + [pltpu.SemaphoreType.DMA((2,))],
        compiler_params=params(61),
        name="pack_key",
    )(keys, values)
    to_query = pl.pallas_call(
        functools.partial(pack_query_kernel, scale),
        out_shape=shape(16, 416, 128),
        in_specs=[pl.BlockSpec(memory_space=pltpu.SMEM)] + [hbm] * 5,
        out_specs=vmem()[0],
        scratch_shapes=[pltpu.VMEM((4, 128, 128), BF16)] * 3
        + [pltpu.VMEM((4, 4, 128), F32), pltpu.VMEM((4, 32, 2048), BF16), pltpu.SemaphoreType.DMA((5,))],
        compiler_params=params(61),
        name="pack_query",
    )(which, queries, out_grad, outputs, logsumexp, bias)
    got_key = lax.all_to_all(to_key, KEY_GROUP, 0, 0)
    got_query = lax.all_to_all(to_query, QUERY_GROUP, 0, 0)
    dq_parts, dkv_parts, db_parts = pl.pallas_call(
        functools.partial(attend_kernel, scale),
        out_shape=(shape(16, 128, 128), shape(16, 256, 128), shape(8, 256, 128)),
        in_specs=vmem(2),
        out_specs=tuple(vmem(3)),
        scratch_shapes=[pltpu.VMEM((512, 512), F32), pltpu.VMEM((512, 512), F32)],
        compiler_params=params(),
        name="attend",
    )(got_query, got_key)
    db = lax.all_to_all(db_parts, "z", 0, 0)
    db = jnp.sum(db.astype(F32), axis=0)
    db = lax.ppermute(db, ROW + ("xh", "yl"), bias_moves())
    db = db.reshape(2, 128, 2, 64).transpose(2, 0, 1, 3).reshape(4, 128, 64)
    bias_grad = lax.all_to_all(db, ("c", "yl"), 0, 0)
    dkv = lax.all_to_all(dkv_parts, KEY_GROUP, 0, 0)
    dq = lax.all_to_all(dq_parts, QUERY_GROUP, 0, 0)
    query_grad, key_grad, value_grad = pl.pallas_call(
        unpack_kernel,
        out_shape=(shape(4, 128, 128),) * 3,
        in_specs=vmem(2),
        out_specs=tuple(vmem(3)),
        compiler_params=params(),
        name="unpack",
    )(dq, dkv)
    return query_grad, key_grad, value_grad, bias_grad


def solution(mesh):
    fine = Mesh(mesh.devices.reshape(2, 8, 2, 2, 4, 2), ROW + BLK)
    rows = P(ROW, BLK, None)
    in_specs = (rows, rows, rows, P(None, BLK, None), rows, rows, P(ROW, None, BLK))
    out_specs = (rows, rows, rows, P(None, BLK, ROW))
    return jax.shard_map(body, mesh=fine, in_specs=in_specs, out_specs=out_specs, check_vma=False)
```

```python
import functools

import jax
import jax.numpy as jnp
from jax import lax
from jax.experimental import pallas as pl
from jax.experimental.pallas import tpu as pltpu
from jax.sharding import Mesh
from jax.sharding import PartitionSpec as P

ROW = ("xl", "z", "c")
BLK = ("xh", "yh", "yl")
QUERY_GROUP = ("xl", "c", "xh", "yl")
KEY_GROUP = ("xl", "c", "yh")
LOG2E = 1.4426950408889634
AUG = 16
F32, BF16 = jnp.float32, jnp.bfloat16


def three_parts(x):
    high = x.astype(BF16).astype(F32)
    rest = x - high
    mid = rest.astype(BF16).astype(F32)
    return high, mid, rest - mid


def fetch(pairs, sems):
    copies = [pltpu.make_async_copy(src, dst, sems.at[at]) for at, (src, dst) in enumerate(pairs)]
    for copy in copies:
        copy.start()
    return copies


def turned(x):
    return x.astype(F32).T.astype(BF16)


def pack_key_kernel(k_hbm, v_hbm, to_key_ref, k_ref, v_ref, sems):
    copies = fetch(((k_hbm, k_ref), (v_hbm, v_ref)), sems)
    for copy in copies:
        copy.wait()
    for i in range(4):
        k_t, v_t = turned(k_ref[i]), turned(v_ref[i])
        for h in range(4):
            part = slice(h * 32, h * 32 + 32)
            for b in range(4):
                to_key_ref[h * 4 + b, i * 64 : i * 64 + 32, :] = k_t[part]
                to_key_ref[h * 4 + b, i * 64 + 32 : i * 64 + 64, :] = v_t[part]


def pack_query_kernel(
    scale, which_ref, q_hbm, g_hbm, o_hbm, l_hbm, bias_hbm, to_query_ref, q_ref, g_ref, o_ref, l_ref, bias_ref, sems
):
    quarter = pl.multiple_of(which_ref[0] * 32, 32)
    copies = fetch(
        (
            (q_hbm, q_ref),
            (g_hbm, g_ref),
            (o_hbm, o_ref),
            (l_hbm, l_ref),
            (bias_hbm.at[:, pl.ds(quarter, 32), :], bias_ref),
        ),
        sems,
    )
    lines = lax.broadcasted_iota(jnp.int32, (AUG, 128), 0)
    for copy in copies[:4]:
        copy.wait()
    for pair in range(2):
        extra = [jnp.zeros((AUG, 128), F32)] * 4
        for n in range(2):
            i = pair * 2 + n
            q_t = turned(q_ref[i])
            g_f = g_ref[i].astype(F32)
            gg = (g_f * o_ref[i].astype(F32)).T
            g_t = g_f.T.astype(BF16)
            for h in range(4):
                part = slice(h * 32, h * 32 + 32)
                offset = l_ref[i, h : h + 1, :] * (-1.0 / scale)
                delta = -jnp.sum(gg[part], axis=0, keepdims=True)
                for at, piece in enumerate(three_parts(offset) + three_parts(delta)):
                    extra[h] = jnp.where(lines == n * 6 + at, piece, extra[h])
                for a in range(4):
                    to_query_ref[h * 4 + a, i * 64 : i * 64 + 32, :] = q_t[part]
                    to_query_ref[h * 4 + a, i * 64 + 32 : i * 64 + 64, :] = g_t[part]
        for h in range(4):
            for a in range(4):
                to_query_ref[h * 4 + a, 256 + pair * 16 : 272 + pair * 16, :] = extra[h].astype(BF16)
    copies[4].wait()
    for h in range(4):
        for a in range(4):
            for yh in range(4):
                block = (a // 2) * 8 + yh * 2 + a % 2
                to_query_ref[h * 4 + a, 288 + yh * 32 : 320 + yh * 32, :] = bias_ref[
                    h, :, block * 128 : block * 128 + 128
                ]


def attend_kernel(scale, yh_ref, jq_ref, kv_ref, dq_ref, dkv0_ref, dkv1_ref, dkv2_ref, dkv3_ref, db_ref, bias_s, acc_s):
    dkv_refs = (dkv0_ref, dkv1_ref, dkv2_ref, dkv3_ref)
    owner = [lax.rem(yh_ref[0] + p, 4) for p in range(4)]
    for a in range(4):
        for s in range(4):
            for p in range(4):
                bias_s[a * 128 + s * 32 : a * 128 + s * 32 + 32, p * 128 : p * 128 + 128] = (
                    jq_ref[s * 4 + a, pl.ds(pl.multiple_of(288 + owner[p] * 32, 32), 32), :].astype(F32) * LOG2E
                )
    acc_s[...] = jnp.zeros_like(acc_s)
    lines = lax.broadcasted_iota(jnp.int32, (AUG, 512), 0)
    ones = [
        jnp.where((lines >= first) & (lines < first + 3), 1.0, 0.0).astype(BF16) for first in (0, 3, 6, 9)
    ]

    def four_rows(s, carry):
        base = s * 4
        for i in range(4):
            first = i * 64
            at = 256 + (i // 2) * 16
            q_t, g_t, extra = (
                jnp.concatenate([jq_ref[base + a, start : start + size, :] for a in range(4)], axis=1)
                for start, size in ((first, 32), (first + 32, 32), (at, 16))
            )
            k_t, v_t = (
                jnp.concatenate([kv_ref[base + owner[p], start : start + 32, :] for p in range(4)], axis=1)
                for start in (first, first + 32)
            )
            q_rows = jnp.concatenate([q_t, extra], axis=0).T
            g_rows = jnp.concatenate([g_t, extra], axis=0).T
            k_aug = jnp.concatenate([k_t, ones[(i % 2) * 2]], axis=0)
            v_aug = jnp.concatenate([v_t, ones[(i % 2) * 2 + 1]], axis=0)
            scores = jnp.dot(q_rows, k_aug, preferred_element_type=F32)
            prob_grad = jnp.dot(g_rows, v_aug, preferred_element_type=F32)
            probs = jnp.exp2(scores * (scale * LOG2E) + bias_s[...])
            score_grad = probs * prob_grad
            acc_s[...] += score_grad
            low = score_grad.astype(BF16)
            dv = jnp.dot(g_t, probs.astype(BF16), preferred_element_type=F32).astype(BF16)
            dk = (jnp.dot(q_t, low, preferred_element_type=F32) * scale).astype(BF16)
            dq = (jnp.dot(low, k_t.T, preferred_element_type=F32).T * scale).astype(BF16)
            for b in range(4):
                block = slice(b * 128, b * 128 + 128)
                dq_ref[base + b, i * 32 : i * 32 + 32, :] = dq[:, block]
                dkv_refs[b][s, first : first + 32, :] = dk[:, block]
                dkv_refs[b][s, first + 32 : first + 64, :] = dv[:, block]
        return carry

    lax.fori_loop(0, 4, four_rows, 0)
    for p in range(4):
        for half in range(2):
            db_ref[owner[p] * 2 + half] = acc_s[half * 256 : half * 256 + 256, p * 128 : p * 128 + 128].astype(BF16)


def unpack_kernel(q_ref, kv_ref, dq_ref, dk_ref, dv_ref):
    for i in range(4):
        heads = []
        for h in range(4):
            parts = [q_ref[h * 4 + a, i * 32 : i * 32 + 32, :].astype(F32) for a in range(4)]
            heads.append(parts[0] + parts[1] + parts[2] + parts[3])
        dq_ref[i] = jnp.concatenate(heads, axis=0).T.astype(BF16)
        for first, out in ((0, dk_ref), (32, dv_ref)):
            at = i * 64 + first
            out[i] = turned(jnp.concatenate([kv_ref[h, at : at + 32, :] for h in range(4)], axis=0))


def vmem(n=1):
    return [pl.BlockSpec(memory_space=pltpu.VMEM)] * n


def params(mib=40):
    return pltpu.CompilerParams(vmem_limit_bytes=mib * 2**20)


def bias_moves():
    pairs = []
    for xl in range(2):
        for z in range(8):
            for c in range(2):
                for xh in range(2):
                    for yl in range(2):
                        source = (((xl * 8 + z) * 2 + c) * 2 + xh) * 2 + yl
                        target = (((xh * 8 + (z // 2) * 2 + yl) * 2 + xl) * 2 + z % 2) * 2 + c
                        pairs.append((source, target))
    return pairs


def body(queries, keys, values, bias, out_grad, outputs, logsumexp):
    scale = 32 ** (-0.5)
    shape = lambda *s: jax.ShapeDtypeStruct(s, BF16)
    which = (lax.axis_index("xl") * 2 + lax.axis_index("c")).astype(jnp.int32).reshape(1)
    hbm = pl.BlockSpec(memory_space=pltpu.HBM)
    to_key = pl.pallas_call(
        pack_key_kernel,
        out_shape=shape(16, 256, 128),
        in_specs=[hbm] * 2,
        out_specs=vmem()[0],
        scratch_shapes=[pltpu.VMEM((4, 128, 128), BF16)] * 2 + [pltpu.SemaphoreType.DMA((2,))],
        compiler_params=params(61),
        name="pack_key",
    )(keys, values)
    to_query = pl.pallas_call(
        functools.partial(pack_query_kernel, scale),
        out_shape=shape(16, 416, 128),
        in_specs=[pl.BlockSpec(memory_space=pltpu.SMEM)] + [hbm] * 5,
        out_specs=vmem()[0],
        scratch_shapes=[pltpu.VMEM((4, 128, 128), BF16)] * 3
        + [pltpu.VMEM((4, 4, 128), F32), pltpu.VMEM((4, 32, 2048), BF16), pltpu.SemaphoreType.DMA((5,))],
        compiler_params=params(61),
        name="pack_query",
    )(which, queries, out_grad, outputs, logsumexp, bias)
    got_key = lax.all_to_all(to_key, KEY_GROUP, 0, 0)
    got_query = lax.all_to_all(to_query, QUERY_GROUP, 0, 0)
    yh = lax.axis_index("yh").astype(jnp.int32).reshape(1)
    dq_parts, *dkv_parts, db_parts = pl.pallas_call(
        functools.partial(attend_kernel, scale),
        out_shape=(shape(16, 128, 128),) + (shape(4, 256, 128),) * 4 + (shape(8, 256, 128),),
        in_specs=[pl.BlockSpec(memory_space=pltpu.SMEM)] + vmem(2),
        out_specs=tuple(vmem(6)),
        scratch_shapes=[pltpu.VMEM((512, 512), F32), pltpu.VMEM((512, 512), F32)],
        compiler_params=params(),
        name="attend",
    )(yh, got_query, got_key)
    dkv = [dkv_parts[0]] + [
        lax.ppermute(dkv_parts[p], "yh", [(n, (n + p) % 4) for n in range(4)]) for p in (2, 1, 3)
    ]
    db = lax.all_to_all(db_parts, "z", 0, 0)
    db = jnp.sum(db.astype(F32), axis=0)
    db = lax.ppermute(db, ROW + ("xh", "yl"), bias_moves())
    db = db.reshape(2, 128, 2, 64).transpose(2, 0, 1, 3).reshape(4, 128, 64)
    bias_grad = lax.all_to_all(db, ("c", "yl"), 0, 0)
    dq = lax.all_to_all(dq_parts, QUERY_GROUP, 0, 0)
    dkv, dq, bias_grad = lax.optimization_barrier((dkv, dq, bias_grad))
    dkv = sum(part.astype(F32) for part in dkv).astype(BF16)
    dkv = lax.all_to_all(dkv, ("xl", "c"), 0, 0)
    query_grad, key_grad, value_grad = pl.pallas_call(
        unpack_kernel,
        out_shape=(shape(4, 128, 128),) * 3,
        in_specs=vmem(2),
        out_specs=tuple(vmem(3)),
        compiler_params=params(),
        name="unpack",
    )(dq, dkv)
    return query_grad, key_grad, value_grad, bias_grad


def solution(mesh):
    fine = Mesh(mesh.devices.reshape(2, 8, 2, 2, 4, 2), ROW + BLK)
    rows = P(ROW, BLK, None)
    in_specs = (rows, rows, rows, P(None, BLK, None), rows, rows, P(ROW, None, BLK))
    out_specs = (rows, rows, rows, P(None, BLK, ROW))
    return jax.shard_map(body, mesh=fine, in_specs=in_specs, out_specs=out_specs, check_vma=False)
```

```python
import functools

import jax
import jax.numpy as jnp
from jax import lax
from jax.experimental import pallas as pl
from jax.experimental.pallas import tpu as pltpu
from jax.sharding import Mesh
from jax.sharding import PartitionSpec as P

ROW = ("xl", "z", "c")
BLK = ("xh", "yh", "yl")
QUERY_GROUP = ("xl", "c", "xh", "yl")
KEY_GROUP = ("xl", "c", "yh")
LOG2E = 1.4426950408889634
AUG = 16
F32, BF16 = jnp.float32, jnp.bfloat16


def three_parts(x):
    high = x.astype(BF16).astype(F32)
    rest = x - high
    mid = rest.astype(BF16).astype(F32)
    return high, mid, rest - mid


def fetch(pairs, sems):
    copies = [pltpu.make_async_copy(src, dst, sems.at[at]) for at, (src, dst) in enumerate(pairs)]
    for copy in copies:
        copy.start()
    return copies


def turned(x):
    return x.astype(F32).T.astype(BF16)


def pack_key_kernel(k_hbm, v_hbm, to_key_ref, k_ref, v_ref, sems):
    copies = fetch(((k_hbm, k_ref), (v_hbm, v_ref)), sems)
    for copy in copies:
        copy.wait()
    for i in range(4):
        k_t, v_t = turned(k_ref[i]), turned(v_ref[i])
        for h in range(4):
            part = slice(h * 32, h * 32 + 32)
            for b in range(4):
                to_key_ref[h * 4 + b, i * 64 : i * 64 + 32, :] = k_t[part]
                to_key_ref[h * 4 + b, i * 64 + 32 : i * 64 + 64, :] = v_t[part]


def pack_query_kernel(
    scale, which_ref, q_hbm, g_hbm, o_hbm, l_hbm, bias_hbm, to_query_ref, q_ref, g_ref, o_ref, l_ref, bias_ref, sems
):
    quarter = pl.multiple_of(which_ref[0] * 32, 32)
    copies = fetch(
        (
            (q_hbm, q_ref),
            (g_hbm, g_ref),
            (o_hbm, o_ref),
            (l_hbm, l_ref),
            (bias_hbm.at[:, pl.ds(quarter, 32), :], bias_ref),
        ),
        sems,
    )
    lines = lax.broadcasted_iota(jnp.int32, (AUG, 128), 0)
    for copy in copies[:4]:
        copy.wait()
    for pair in range(2):
        extra = [jnp.zeros((AUG, 128), F32)] * 4
        for n in range(2):
            i = pair * 2 + n
            q_t = turned(q_ref[i])
            g_f = g_ref[i].astype(F32)
            gg = (g_f * o_ref[i].astype(F32)).T
            g_t = g_f.T.astype(BF16)
            for h in range(4):
                part = slice(h * 32, h * 32 + 32)
                offset = l_ref[i, h : h + 1, :] * (-1.0 / scale)
                delta = -jnp.sum(gg[part], axis=0, keepdims=True)
                for at, piece in enumerate(three_parts(offset) + three_parts(delta)):
                    extra[h] = jnp.where(lines == n * 6 + at, piece, extra[h])
                for a in range(4):
                    to_query_ref[h * 4 + a, i * 64 : i * 64 + 32, :] = q_t[part]
                    to_query_ref[h * 4 + a, i * 64 + 32 : i * 64 + 64, :] = g_t[part]
        for h in range(4):
            for a in range(4):
                to_query_ref[h * 4 + a, 256 + pair * 16 : 272 + pair * 16, :] = extra[h].astype(BF16)
    copies[4].wait()
    for h in range(4):
        for a in range(4):
            for yh in range(4):
                block = (a // 2) * 8 + yh * 2 + a % 2
                to_query_ref[h * 4 + a, 288 + yh * 32 : 320 + yh * 32, :] = bias_ref[
                    h, :, block * 128 : block * 128 + 128
                ]


def attend_kernel(scale, yh_ref, jq_ref, kv_ref, dq_ref, dkv0_ref, dkv1_ref, dk2_ref, dv2_ref, dkv3_ref, db_ref, bias_s, acc_s):
    dkv_refs = (dkv0_ref, dkv1_ref, None, dkv3_ref)
    owner = [lax.rem(yh_ref[0] + p, 4) for p in range(4)]
    for a in range(4):
        for s in range(4):
            for p in range(4):
                bias_s[a * 128 + s * 32 : a * 128 + s * 32 + 32, p * 128 : p * 128 + 128] = (
                    jq_ref[s * 4 + a, pl.ds(pl.multiple_of(288 + owner[p] * 32, 32), 32), :].astype(F32) * LOG2E
                )
    acc_s[...] = jnp.zeros_like(acc_s)
    lines = lax.broadcasted_iota(jnp.int32, (AUG, 512), 0)
    ones = [
        jnp.where((lines >= first) & (lines < first + 3), 1.0, 0.0).astype(BF16) for first in (0, 3, 6, 9)
    ]

    def four_rows(s, carry):
        base = s * 4
        for i in range(4):
            first = i * 64
            at = 256 + (i // 2) * 16
            q_t, g_t, extra = (
                jnp.concatenate([jq_ref[base + a, start : start + size, :] for a in range(4)], axis=1)
                for start, size in ((first, 32), (first + 32, 32), (at, 16))
            )
            k_t, v_t = (
                jnp.concatenate([kv_ref[base + owner[p], start : start + 32, :] for p in range(4)], axis=1)
                for start in (first, first + 32)
            )
            q_rows = jnp.concatenate([q_t, extra], axis=0).T
            g_rows = jnp.concatenate([g_t, extra], axis=0).T
            k_aug = jnp.concatenate([k_t, ones[(i % 2) * 2]], axis=0)
            v_aug = jnp.concatenate([v_t, ones[(i % 2) * 2 + 1]], axis=0)
            scores = jnp.dot(q_rows, k_aug, preferred_element_type=F32)
            prob_grad = jnp.dot(g_rows, v_aug, preferred_element_type=F32)
            probs = jnp.exp2(scores * (scale * LOG2E) + bias_s[...])
            score_grad = probs * prob_grad
            acc_s[...] += score_grad
            low = score_grad.astype(BF16)
            dv = jnp.dot(g_t, probs.astype(BF16), preferred_element_type=F32).astype(BF16)
            dk = (jnp.dot(q_t, low, preferred_element_type=F32) * scale).astype(BF16)
            dq = (jnp.dot(low, k_t.T, preferred_element_type=F32).T * scale).astype(BF16)
            for b in range(4):
                block = slice(b * 128, b * 128 + 128)
                dq_ref[base + b, i * 32 : i * 32 + 32, :] = dq[:, block]
                low_at, high_at = slice(i * 32, i * 32 + 32), slice(128 + i * 32, 160 + i * 32)
                if b == 2:
                    dk2_ref[s, low_at, :] = dk[:, block]
                    dv2_ref[s, low_at, :] = dv[:, block]
                else:
                    dkv_refs[b][s, low_at, :] = dk[:, block]
                    dkv_refs[b][s, high_at, :] = dv[:, block]
        return carry

    lax.fori_loop(0, 4, four_rows, 0)
    for p in range(4):
        for xh in range(2):
            for yl in range(2):
                j = (xh * 2 + yl) * 128
                db_ref[owner[p] * 4 + yl * 2 + xh] = acc_s[j : j + 128, p * 128 : p * 128 + 128].astype(BF16)


def fold_kernel(up_ref, up_more_ref, down_ref, down_more_ref, up_out_ref, down_out_ref):
    for s in range(4):
        up_out_ref[s, :128, :] = (up_ref[s, :128, :].astype(F32) + up_more_ref[s].astype(F32)).astype(BF16)
        up_out_ref[s, 128:, :] = up_ref[s, 128:, :]
        down_out_ref[s, :128, :] = down_ref[s, :128, :]
        down_out_ref[s, 128:, :] = (down_ref[s, 128:, :].astype(F32) + down_more_ref[s].astype(F32)).astype(BF16)


def join_kernel(own_ref, up_ref, down_ref, db_ref, out_ref):
    for s in range(4):
        total = own_ref[s].astype(F32) + up_ref[s].astype(F32) + down_ref[s].astype(F32)
        out_ref[s, :256, :] = total.astype(BF16)
    first_half = lax.broadcasted_iota(jnp.int32, (128, 128), 1) < 64
    for xl in range(2):
        whole = db_ref[xl]
        high = whole.astype(BF16).astype(F32)
        low = whole - high
        out_ref[xl * 2, 256:, :] = jnp.where(first_half, high, pltpu.roll(low, 64, 1)).astype(BF16)
        out_ref[xl * 2 + 1, 256:, :] = jnp.where(first_half, pltpu.roll(high, 64, 1), low).astype(BF16)


def unpack_kernel(q_ref, kv_ref, dq_ref, dk_ref, dv_ref, db_ref):
    for h in range(4):
        parts = kv_ref[h, 256:, :].astype(F32)
        db_ref[h] = (parts + pltpu.roll(parts, 64, 1)).T[:64]
    for i in range(4):
        heads = []
        for h in range(4):
            parts = [q_ref[h * 4 + a, i * 32 : i * 32 + 32, :].astype(F32) for a in range(4)]
            heads.append(parts[0] + parts[1] + parts[2] + parts[3])
        dq_ref[i] = jnp.concatenate(heads, axis=0).T.astype(BF16)
        for first, out in ((0, dk_ref), (128, dv_ref)):
            at = i * 32 + first
            out[i] = turned(jnp.concatenate([kv_ref[h, at : at + 32, :] for h in range(4)], axis=0))


def vmem(n=1):
    return [pl.BlockSpec(memory_space=pltpu.VMEM)] * n


def params(mib=40):
    return pltpu.CompilerParams(vmem_limit_bytes=mib * 2**20)


def swaps():
    return [(z * 2 + yl, ((z // 2) * 2 + yl) * 2 + z % 2) for z in range(8) for yl in range(2)]


def along(value, steps):
    return lax.ppermute(value, "yh", [(n, (n + steps) % 4) for n in range(4)])


def body(queries, keys, values, bias, out_grad, outputs, logsumexp):
    scale = 32 ** (-0.5)
    shape = lambda *s: jax.ShapeDtypeStruct(s, BF16)
    which = (lax.axis_index("xl") * 2 + lax.axis_index("c")).astype(jnp.int32).reshape(1)
    hbm = pl.BlockSpec(memory_space=pltpu.HBM)
    to_key = pl.pallas_call(
        pack_key_kernel,
        out_shape=shape(16, 256, 128),
        in_specs=[hbm] * 2,
        out_specs=vmem()[0],
        scratch_shapes=[pltpu.VMEM((4, 128, 128), BF16)] * 2 + [pltpu.SemaphoreType.DMA((2,))],
        compiler_params=params(61),
        name="pack_key",
    )(keys, values)
    to_query = pl.pallas_call(
        functools.partial(pack_query_kernel, scale),
        out_shape=shape(16, 416, 128),
        in_specs=[pl.BlockSpec(memory_space=pltpu.SMEM)] + [hbm] * 5,
        out_specs=vmem()[0],
        scratch_shapes=[pltpu.VMEM((4, 128, 128), BF16)] * 3
        + [pltpu.VMEM((4, 4, 128), F32), pltpu.VMEM((4, 32, 2048), BF16), pltpu.SemaphoreType.DMA((5,))],
        compiler_params=params(61),
        name="pack_query",
    )(which, queries, out_grad, outputs, logsumexp, bias)
    got_key = lax.all_to_all(to_key, KEY_GROUP, 0, 0)
    got_query = lax.all_to_all(to_query, QUERY_GROUP, 0, 0)
    yh = lax.axis_index("yh").astype(jnp.int32).reshape(1)
    dq_parts, own, up, dk_far, dv_far, down, db_parts = pl.pallas_call(
        functools.partial(attend_kernel, scale),
        out_shape=(shape(16, 128, 128),)
        + (shape(4, 256, 128),) * 2
        + (shape(4, 128, 128),) * 2
        + (shape(4, 256, 128), shape(16, 128, 128)),
        in_specs=[pl.BlockSpec(memory_space=pltpu.SMEM)] + vmem(2),
        out_specs=tuple(vmem(7)),
        scratch_shapes=[pltpu.VMEM((512, 512), F32), pltpu.VMEM((512, 512), F32)],
        compiler_params=params(),
        name="attend",
    )(yh, got_query, got_key)
    up_more, down_more = along(dk_far, 1), along(dv_far, -1)
    up, down = pl.pallas_call(
        fold_kernel,
        out_shape=(shape(4, 256, 128),) * 2,
        in_specs=vmem(4),
        out_specs=tuple(vmem(2)),
        compiler_params=params(),
        name="fold",
    )(up, up_more, down, down_more)
    db = lax.all_to_all(db_parts, ("z", "xh"), 0, 0)
    up, down, db, dq_parts = lax.optimization_barrier((up, down, db, dq_parts))
    up, down = along(up, 1), along(down, -1)
    db = jnp.sum(db.reshape(8, 2, 128, 128).astype(F32), axis=0)
    db = lax.ppermute(db, ("z", "yl"), swaps())
    dq = lax.all_to_all(dq_parts, QUERY_GROUP, 0, 0)
    up, down, db, dq = lax.optimization_barrier((up, down, db, dq))
    joined = pl.pallas_call(
        join_kernel,
        out_shape=shape(4, 384, 128),
        in_specs=vmem(4),
        out_specs=vmem()[0],
        compiler_params=params(),
        name="join",
    )(own, up, down, db)
    joined = lax.all_to_all(joined, ("xl", "c"), 0, 0)
    query_grad, key_grad, value_grad, bias_grad = pl.pallas_call(
        unpack_kernel,
        out_shape=(shape(4, 128, 128),) * 3 + (jax.ShapeDtypeStruct((4, 64, 128), F32),),
        in_specs=vmem(2),
        out_specs=tuple(vmem(4)),
        compiler_params=params(),
        name="unpack",
    )(dq, joined)
    return query_grad, key_grad, value_grad, bias_grad.transpose(0, 2, 1)


def solution(mesh):
    fine = Mesh(mesh.devices.reshape(2, 8, 2, 2, 4, 2), ROW + BLK)
    rows = P(ROW, BLK, None)
    in_specs = (rows, rows, rows, P(None, BLK, None), rows, rows, P(ROW, None, BLK))
    out_specs = (rows, rows, rows, P(None, BLK, ROW))
    return jax.shard_map(body, mesh=fine, in_specs=in_specs, out_specs=out_specs, check_vma=False)
```

```python
import functools

import jax
import jax.numpy as jnp
from jax import lax
from jax.experimental import pallas as pl
from jax.experimental.pallas import tpu as pltpu
from jax.sharding import Mesh
from jax.sharding import PartitionSpec as P

ROW = ("xl", "z", "c")
BLK = ("xh", "yh", "yl")
QUERY_GROUP = ("xl", "c", "xh", "yl")
KEY_GROUP = ("xl", "c", "yh")
LOG2E = 1.4426950408889634
AUG = 16
F32, BF16 = jnp.float32, jnp.bfloat16


def two_parts(x):
    high = x.astype(BF16).astype(F32)
    return high, x - high


def fetch(pairs, sems):
    copies = [pltpu.make_async_copy(src, dst, sems.at[at]) for at, (src, dst) in enumerate(pairs)]
    for copy in copies:
        copy.start()
    return copies


def turned(x):
    return x.astype(F32).T.astype(BF16)


def pack_key_kernel(k_hbm, v_hbm, to_key_ref, k_ref, v_ref, sems):
    copies = fetch(((k_hbm, k_ref), (v_hbm, v_ref)), sems)
    for copy in copies:
        copy.wait()
    for i in range(4):
        k_t, v_t = turned(k_ref[i]), turned(v_ref[i])
        for h in range(4):
            part = slice(h * 32, h * 32 + 32)
            for b in range(4):
                to_key_ref[h * 4 + b, i * 64 : i * 64 + 32, :] = k_t[part]
                to_key_ref[h * 4 + b, i * 64 + 32 : i * 64 + 64, :] = v_t[part]


def pack_query_kernel(
    scale, which_ref, q_hbm, g_hbm, o_hbm, l_hbm, bias_hbm, to_query_ref, q_ref, g_ref, o_ref, l_ref, bias_ref, sems
):
    quarter = pl.multiple_of(which_ref[0] * 32, 32)
    copies = fetch(
        (
            (q_hbm, q_ref),
            (g_hbm, g_ref),
            (o_hbm, o_ref),
            (l_hbm, l_ref),
            (bias_hbm.at[:, pl.ds(quarter, 32), :], bias_ref),
        ),
        sems,
    )
    lines = lax.broadcasted_iota(jnp.int32, (AUG, 128), 0)
    for copy in copies[:4]:
        copy.wait()
    extra = [jnp.zeros((AUG, 128), F32)] * 4
    for i in range(4):
        q_t = turned(q_ref[i])
        g_f = g_ref[i].astype(F32)
        gg = (g_f * o_ref[i].astype(F32)).T
        g_t = g_f.T.astype(BF16)
        for h in range(4):
            part = slice(h * 32, h * 32 + 32)
            offset = l_ref[i, h : h + 1, :] * (-1.0 / scale)
            delta = -jnp.sum(gg[part], axis=0, keepdims=True)
            for at, piece in enumerate(two_parts(offset) + two_parts(delta)):
                extra[h] = jnp.where(lines == i * 4 + at, piece, extra[h])
            for a in range(4):
                to_query_ref[h * 4 + a, i * 64 : i * 64 + 32, :] = q_t[part]
                to_query_ref[h * 4 + a, i * 64 + 32 : i * 64 + 64, :] = g_t[part]
    for h in range(4):
        for a in range(4):
            to_query_ref[h * 4 + a, 256:272, :] = extra[h].astype(BF16)
    copies[4].wait()
    for h in range(4):
        for a in range(4):
            for yh in range(4):
                block = (a // 2) * 8 + yh * 2 + a % 2
                to_query_ref[h * 4 + a, 272 + yh * 32 : 304 + yh * 32, :] = bias_ref[
                    h, :, block * 128 : block * 128 + 128
                ]


def attend_kernel(scale, yh_ref, jq_ref, kv_ref, dq_ref, dkv0_ref, dkv1_ref, dk2_ref, dv2_ref, dkv3_ref, db_ref, bias_s, acc_s):
    dkv_refs = (dkv0_ref, dkv1_ref, None, dkv3_ref)
    owner = [lax.rem(yh_ref[0] + p, 4) for p in range(4)]
    for a in range(4):
        for s in range(4):
            for p in range(4):
                bias_s[a * 128 + s * 32 : a * 128 + s * 32 + 32, p * 128 : p * 128 + 128] = (
                    jq_ref[s * 4 + a, pl.ds(pl.multiple_of(272 + owner[p] * 32, 16), 32), :].astype(F32) * LOG2E
                )
    acc_s[...] = jnp.zeros_like(acc_s)
    lines = lax.broadcasted_iota(jnp.int32, (AUG, 512), 0)
    ones = [
        jnp.where((lines >= first) & (lines < first + 2), 1.0, 0.0).astype(BF16) for first in range(0, 16, 2)
    ]

    def four_rows(s, carry):
        base = s * 4
        for i in range(4):
            first = i * 64
            q_t, g_t, extra = (
                jnp.concatenate([jq_ref[base + a, start : start + size, :] for a in range(4)], axis=1)
                for start, size in ((first, 32), (first + 32, 32), (256, 16))
            )
            k_t, v_t = (
                jnp.concatenate([kv_ref[base + owner[p], start : start + 32, :] for p in range(4)], axis=1)
                for start in (first, first + 32)
            )
            q_rows = jnp.concatenate([q_t, extra], axis=0).T
            g_rows = jnp.concatenate([g_t, extra], axis=0).T
            k_aug = jnp.concatenate([k_t, ones[i * 2]], axis=0)
            v_aug = jnp.concatenate([v_t, ones[i * 2 + 1]], axis=0)
            scores = jnp.dot(q_rows, k_aug, preferred_element_type=F32)
            prob_grad = jnp.dot(g_rows, v_aug, preferred_element_type=F32)
            probs = jnp.exp2(scores * (scale * LOG2E) + bias_s[...])
            score_grad = probs * prob_grad
            acc_s[...] += score_grad
            low = score_grad.astype(BF16)
            dv = jnp.dot(g_t, probs.astype(BF16), preferred_element_type=F32).astype(BF16)
            dk = (jnp.dot(q_t, low, preferred_element_type=F32) * scale).astype(BF16)
            dq = (jnp.dot(low, k_t.T, preferred_element_type=F32).T * scale).astype(BF16)
            for b in range(4):
                block = slice(b * 128, b * 128 + 128)
                dq_ref[base + b, i * 32 : i * 32 + 32, :] = dq[:, block]
                low_at, high_at = slice(i * 32, i * 32 + 32), slice(128 + i * 32, 160 + i * 32)
                if b == 2:
                    dk2_ref[s, low_at, :] = dk[:, block]
                    dv2_ref[s, low_at, :] = dv[:, block]
                else:
                    dkv_refs[b][s, low_at, :] = dk[:, block]
                    dkv_refs[b][s, high_at, :] = dv[:, block]
        return carry

    lax.fori_loop(0, 4, four_rows, 0)
    for p in range(4):
        for xh in range(2):
            for yl in range(2):
                j = (xh * 2 + yl) * 128
                piece = acc_s[j : j + 128, p * 128 : p * 128 + 128].astype(BF16)
                for zl in range(2):
                    db_ref[owner[p] * 8 + zl * 4 + xh * 2 + yl] = piece


def fold_kernel(up_ref, up_more_ref, down_ref, down_more_ref, up_out_ref, down_out_ref):
    for s in range(4):
        up_out_ref[s, :128, :] = (up_ref[s, :128, :].astype(F32) + up_more_ref[s].astype(F32)).astype(BF16)
        up_out_ref[s, 128:, :] = up_ref[s, 128:, :]
        down_out_ref[s, :128, :] = down_ref[s, :128, :]
        down_out_ref[s, 128:, :] = (down_ref[s, 128:, :].astype(F32) + down_more_ref[s].astype(F32)).astype(BF16)


def join_kernel(zl_ref, own_ref, up_ref, down_ref, db_ref, out_ref):
    for s in range(4):
        total = own_ref[s].astype(F32) + up_ref[s].astype(F32) + down_ref[s].astype(F32)
        out_ref[s, :256, :] = total.astype(BF16)
    first_half = lax.broadcasted_iota(jnp.int32, (128, 128), 1) < 64
    for xl in range(2):
        parts = [db_ref[z * 4 + xl * 2 + zl_ref[0]].astype(F32) for z in range(8)]
        whole = ((parts[0] + parts[1]) + (parts[2] + parts[3])) + ((parts[4] + parts[5]) + (parts[6] + parts[7]))
        high = whole.astype(BF16).astype(F32)
        low = whole - high
        out_ref[xl * 2, 256:, :] = jnp.where(first_half, high, pltpu.roll(low, 64, 1)).astype(BF16)
        out_ref[xl * 2 + 1, 256:, :] = jnp.where(first_half, pltpu.roll(high, 64, 1), low).astype(BF16)


def unpack_query_kernel(q_ref, dq_ref):
    for i in range(4):
        heads = []
        for h in range(4):
            parts = [q_ref[h * 4 + a, i * 32 : i * 32 + 32, :].astype(F32) for a in range(4)]
            heads.append(parts[0] + parts[1] + parts[2] + parts[3])
        dq_ref[i] = jnp.concatenate(heads, axis=0).T.astype(BF16)


def unpack_kernel(kv_ref, dk_ref, dv_ref, db_ref):
    for h in range(4):
        parts = kv_ref[h, 256:, :].astype(F32)
        db_ref[h] = (parts + pltpu.roll(parts, 64, 1)).T[:64]
    for i in range(4):
        for first, out in ((0, dk_ref), (128, dv_ref)):
            at = i * 32 + first
            out[i] = turned(jnp.concatenate([kv_ref[h, at : at + 32, :] for h in range(4)], axis=0))


def vmem(n=1):
    return [pl.BlockSpec(memory_space=pltpu.VMEM)] * n


def params(mib=40):
    return pltpu.CompilerParams(vmem_limit_bytes=mib * 2**20)


def along(value, steps):
    return lax.ppermute(value, "yh", [(n, (n + steps) % 4) for n in range(4)])


def body(queries, keys, values, bias, out_grad, outputs, logsumexp):
    scale = 32 ** (-0.5)
    shape = lambda *s: jax.ShapeDtypeStruct(s, BF16)
    which = (lax.axis_index("xl") * 2 + lax.axis_index("c")).astype(jnp.int32).reshape(1)
    hbm = pl.BlockSpec(memory_space=pltpu.HBM)
    to_key = pl.pallas_call(
        pack_key_kernel,
        out_shape=shape(16, 256, 128),
        in_specs=[hbm] * 2,
        out_specs=vmem()[0],
        scratch_shapes=[pltpu.VMEM((4, 128, 128), BF16)] * 2 + [pltpu.SemaphoreType.DMA((2,))],
        compiler_params=params(61),
        name="pack_key",
    )(keys, values)
    to_query = pl.pallas_call(
        functools.partial(pack_query_kernel, scale),
        out_shape=shape(16, 400, 128),
        in_specs=[pl.BlockSpec(memory_space=pltpu.SMEM)] + [hbm] * 5,
        out_specs=vmem()[0],
        scratch_shapes=[pltpu.VMEM((4, 128, 128), BF16)] * 3
        + [pltpu.VMEM((4, 4, 128), F32), pltpu.VMEM((4, 32, 2048), BF16), pltpu.SemaphoreType.DMA((5,))],
        compiler_params=params(61),
        name="pack_query",
    )(which, queries, out_grad, outputs, logsumexp, bias)
    got_key = lax.all_to_all(to_key, KEY_GROUP, 0, 0)
    got_query = lax.all_to_all(to_query, QUERY_GROUP, 0, 0)
    yh = lax.axis_index("yh").astype(jnp.int32).reshape(1)
    dq_parts, own, up, dk_far, dv_far, down, db_parts = pl.pallas_call(
        functools.partial(attend_kernel, scale),
        out_shape=(shape(16, 128, 128),)
        + (shape(4, 256, 128),) * 2
        + (shape(4, 128, 128),) * 2
        + (shape(4, 256, 128), shape(32, 128, 128)),
        in_specs=[pl.BlockSpec(memory_space=pltpu.SMEM)] + vmem(2),
        out_specs=tuple(vmem(7)),
        scratch_shapes=[pltpu.VMEM((512, 512), F32), pltpu.VMEM((512, 512), F32)],
        compiler_params=params(),
        name="attend",
    )(yh, got_query, got_key)
    up_more, down_more = along(dk_far, 1), along(dv_far, -1)
    up, down = pl.pallas_call(
        fold_kernel,
        out_shape=(shape(4, 256, 128),) * 2,
        in_specs=vmem(4),
        out_specs=tuple(vmem(2)),
        compiler_params=params(),
        name="fold",
    )(up, up_more, down, down_more)
    db = lax.all_to_all(db_parts, ("z", "xh", "yl"), 0, 0)
    up, down, db, dq_parts = lax.optimization_barrier((up, down, db, dq_parts))
    up, down = along(up, 1), along(down, -1)
    dq = lax.all_to_all(dq_parts, QUERY_GROUP, 0, 0)
    up, down, db, dq = lax.optimization_barrier((up, down, db, dq))
    joined = pl.pallas_call(
        join_kernel,
        out_shape=shape(4, 384, 128),
        in_specs=[pl.BlockSpec(memory_space=pltpu.SMEM)] + vmem(4),
        out_specs=vmem()[0],
        compiler_params=params(),
        name="join",
    )(lax.rem(lax.axis_index("z"), 2).astype(jnp.int32).reshape(1), own, up, down, db)
    joined = lax.all_to_all(joined, ("xl", "c"), 0, 0)
    query_grad = pl.pallas_call(
        unpack_query_kernel,
        out_shape=shape(4, 128, 128),
        in_specs=vmem(1),
        out_specs=vmem()[0],
        compiler_params=params(),
        name="unpack_query",
    )(dq)
    key_grad, value_grad, bias_grad = pl.pallas_call(
        unpack_kernel,
        out_shape=(shape(4, 128, 128),) * 2 + (jax.ShapeDtypeStruct((4, 64, 128), F32),),
        in_specs=vmem(1),
        out_specs=tuple(vmem(3)),
        compiler_params=params(),
        name="unpack",
    )(joined)
    return query_grad, key_grad, value_grad, bias_grad.transpose(0, 2, 1)


def solution(mesh):
    fine = Mesh(mesh.devices.reshape(2, 8, 2, 2, 4, 2), ROW + BLK)
    rows = P(ROW, BLK, None)
    in_specs = (rows, rows, rows, P(None, BLK, None), rows, rows, P(ROW, None, BLK))
    out_specs = (rows, rows, rows, P(None, BLK, ROW))
    return jax.shard_map(body, mesh=fine, in_specs=in_specs, out_specs=out_specs, check_vma=False)
```

```python
import functools

import jax
import jax.numpy as jnp
from jax import lax
from jax.experimental import pallas as pl
from jax.experimental.pallas import tpu as pltpu
from jax.sharding import Mesh
from jax.sharding import PartitionSpec as P

ROW = ("xl", "z", "c")
BLK = ("xh", "yh", "yl")
QUERY_GROUP = ("xl", "c", "xh", "yl")
LOG2E = 1.4426950408889634
AUG = 16
F32, BF16 = jnp.float32, jnp.bfloat16


def two_parts(x):
    high = x.astype(BF16).astype(F32)
    return high, x - high


def fetch(pairs, sems):
    copies = [pltpu.make_async_copy(src, dst, sems.at[at]) for at, (src, dst) in enumerate(pairs)]
    for copy in copies:
        copy.start()
    return copies


def turned(x):
    return x.astype(F32).T.astype(BF16)


def pack_key_kernel(k_hbm, v_hbm, to_key_ref, k_ref, v_ref, sems):
    copies = fetch(((k_hbm, k_ref), (v_hbm, v_ref)), sems)
    for copy in copies:
        copy.wait()
    for i in range(4):
        k_t, v_t = turned(k_ref[i]), turned(v_ref[i])
        for h in range(4):
            part = slice(h * 32, h * 32 + 32)
            to_key_ref[h, i * 32 : i * 32 + 32, :] = k_t[part]
            to_key_ref[h, 128 + i * 32 : 160 + i * 32, :] = v_t[part]


def pack_query_kernel(
    scale, which_ref, q_hbm, g_hbm, o_hbm, l_hbm, bias_hbm, to_query_ref, q_ref, g_ref, o_ref, l_ref, bias_ref, sems
):
    quarter = pl.multiple_of(which_ref[0] * 32, 32)
    copies = fetch(
        (
            (q_hbm, q_ref),
            (g_hbm, g_ref),
            (o_hbm, o_ref),
            (l_hbm, l_ref),
            (bias_hbm.at[:, pl.ds(quarter, 32), :], bias_ref),
        ),
        sems,
    )
    lines = lax.broadcasted_iota(jnp.int32, (AUG, 128), 0)
    for copy in copies[:4]:
        copy.wait()
    extra = [jnp.zeros((AUG, 128), F32)] * 4
    for i in range(4):
        q_t = turned(q_ref[i])
        g_f = g_ref[i].astype(F32)
        gg = (g_f * o_ref[i].astype(F32)).T
        g_t = g_f.T.astype(BF16)
        for h in range(4):
            part = slice(h * 32, h * 32 + 32)
            offset = l_ref[i, h : h + 1, :] * (-1.0 / scale)
            delta = -jnp.sum(gg[part], axis=0, keepdims=True)
            for at, piece in enumerate(two_parts(offset) + two_parts(delta)):
                extra[h] = jnp.where(lines == i * 4 + at, piece, extra[h])
            for a in range(4):
                to_query_ref[h * 4 + a, i * 64 : i * 64 + 32, :] = q_t[part]
                to_query_ref[h * 4 + a, i * 64 + 32 : i * 64 + 64, :] = g_t[part]
    for h in range(4):
        for a in range(4):
            to_query_ref[h * 4 + a, 256:272, :] = extra[h].astype(BF16)
    copies[4].wait()
    for h in range(4):
        for a in range(4):
            for yh in range(4):
                block = (a // 2) * 8 + yh * 2 + a % 2
                to_query_ref[h * 4 + a, 272 + yh * 32 : 304 + yh * 32, :] = bias_ref[
                    h, :, block * 128 : block * 128 + 128
                ]


def attend_kernel(
    scale,
    yh_ref,
    jq_ref,
    kv0_ref,
    kv1_ref,
    k2_ref,
    v2_ref,
    kv3_ref,
    dq_ref,
    dkv0_ref,
    dkv1_ref,
    dk2_ref,
    dv2_ref,
    dkv3_ref,
    db_ref,
    bias_s,
    acc_s,
):
    dkv_refs = (dkv0_ref, dkv1_ref, None, dkv3_ref)
    owner = [lax.rem(yh_ref[0] + p, 4) for p in range(4)]
    for a in range(4):
        for s in range(4):
            for p in range(4):
                bias_s[a * 128 + s * 32 : a * 128 + s * 32 + 32, p * 128 : p * 128 + 128] = (
                    jq_ref[s * 4 + a, pl.ds(pl.multiple_of(272 + owner[p] * 32, 16), 32), :].astype(F32) * LOG2E
                )
    acc_s[...] = jnp.zeros_like(acc_s)
    lines = lax.broadcasted_iota(jnp.int32, (AUG, 512), 0)
    ones = [
        jnp.where((lines >= first) & (lines < first + 2), 1.0, 0.0).astype(BF16) for first in range(0, 16, 2)
    ]

    def four_rows(s, carry):
        base = s * 4
        for i in range(4):
            first = i * 64
            q_t, g_t, extra = (
                jnp.concatenate([jq_ref[base + a, start : start + size, :] for a in range(4)], axis=1)
                for start, size in ((first, 32), (first + 32, 32), (256, 16))
            )
            low_at, high_at = slice(i * 32, i * 32 + 32), slice(128 + i * 32, 160 + i * 32)
            k_t = jnp.concatenate(
                [kv0_ref[s, low_at, :], kv1_ref[s, low_at, :], k2_ref[s, low_at, :], kv3_ref[s, low_at, :]], axis=1
            )
            v_t = jnp.concatenate(
                [kv0_ref[s, high_at, :], kv1_ref[s, high_at, :], v2_ref[s, low_at, :], kv3_ref[s, high_at, :]], axis=1
            )
            q_rows = jnp.concatenate([q_t, extra], axis=0).T
            g_rows = jnp.concatenate([g_t, extra], axis=0).T
            k_aug = jnp.concatenate([k_t, ones[i * 2]], axis=0)
            v_aug = jnp.concatenate([v_t, ones[i * 2 + 1]], axis=0)
            scores = jnp.dot(q_rows, k_aug, preferred_element_type=F32)
            prob_grad = jnp.dot(g_rows, v_aug, preferred_element_type=F32)
            probs = jnp.exp2(scores * (scale * LOG2E) + bias_s[...])
            score_grad = probs * prob_grad
            acc_s[...] += score_grad
            low = score_grad.astype(BF16)
            dv = jnp.dot(g_t, probs.astype(BF16), preferred_element_type=F32).astype(BF16)
            dk = (jnp.dot(q_t, low, preferred_element_type=F32) * scale).astype(BF16)
            dq = (jnp.dot(low, k_t.T, preferred_element_type=F32).T * scale).astype(BF16)
            for b in range(4):
                block = slice(b * 128, b * 128 + 128)
                dq_ref[base + b, i * 32 : i * 32 + 32, :] = dq[:, block]
                if b == 2:
                    dk2_ref[s, low_at, :] = dk[:, block]
                    dv2_ref[s, low_at, :] = dv[:, block]
                else:
                    dkv_refs[b][s, low_at, :] = dk[:, block]
                    dkv_refs[b][s, high_at, :] = dv[:, block]
        return carry

    lax.fori_loop(0, 4, four_rows, 0)
    for p in range(4):
        for xh in range(2):
            for yl in range(2):
                j = (xh * 2 + yl) * 128
                piece = acc_s[j : j + 128, p * 128 : p * 128 + 128].astype(BF16)
                db_ref[owner[p] * 4 + yl * 2 + xh] = piece


def fold_kernel(up_ref, up_more_ref, down_ref, down_more_ref, up_out_ref, down_out_ref):
    for s in range(4):
        up_out_ref[s, :128, :] = (up_ref[s, :128, :].astype(F32) + up_more_ref[s].astype(F32)).astype(BF16)
        up_out_ref[s, 128:, :] = up_ref[s, 128:, :]
        down_out_ref[s, :128, :] = down_ref[s, :128, :]
        down_out_ref[s, 128:, :] = (down_ref[s, 128:, :].astype(F32) + down_more_ref[s].astype(F32)).astype(BF16)


def join_kernel(own_ref, up_ref, down_ref, db_ref, out_ref):
    for s in range(4):
        total = own_ref[s].astype(F32) + up_ref[s].astype(F32) + down_ref[s].astype(F32)
        out_ref[s, :256, :] = total.astype(BF16)
    first_half = lax.broadcasted_iota(jnp.int32, (128, 128), 1) < 64
    for xl in range(2):
        whole = db_ref[xl]
        high = whole.astype(BF16).astype(F32)
        low = whole - high
        out_ref[xl * 2, 256:, :] = jnp.where(first_half, high, pltpu.roll(low, 64, 1)).astype(BF16)
        out_ref[xl * 2 + 1, 256:, :] = jnp.where(first_half, pltpu.roll(high, 64, 1), low).astype(BF16)


def unpack_query_kernel(q_ref, dq_ref):
    for i in range(4):
        heads = []
        for h in range(4):
            parts = [q_ref[h * 4 + a, i * 32 : i * 32 + 32, :].astype(F32) for a in range(4)]
            heads.append(parts[0] + parts[1] + parts[2] + parts[3])
        dq_ref[i] = jnp.concatenate(heads, axis=0).T.astype(BF16)


def unpack_kernel(kv_ref, dk_ref, dv_ref, db_ref):
    for h in range(4):
        parts = kv_ref[h, 256:, :].astype(F32)
        db_ref[h] = (parts + pltpu.roll(parts, 64, 1)).T[:64]
    for i in range(4):
        for first, out in ((0, dk_ref), (128, dv_ref)):
            at = i * 32 + first
            out[i] = turned(jnp.concatenate([kv_ref[h, at : at + 32, :] for h in range(4)], axis=0))


def vmem(n=1):
    return [pl.BlockSpec(memory_space=pltpu.VMEM)] * n


def params(mib=40):
    return pltpu.CompilerParams(vmem_limit_bytes=mib * 2**20)


def swaps():
    return [(z * 2 + yl, ((z // 2) * 2 + yl) * 2 + z % 2) for z in range(8) for yl in range(2)]


def along(value, steps):
    return lax.ppermute(value, "yh", [(n, (n + steps) % 4) for n in range(4)])


def body(queries, keys, values, bias, out_grad, outputs, logsumexp):
    scale = 32 ** (-0.5)
    shape = lambda *s: jax.ShapeDtypeStruct(s, BF16)
    which = (lax.axis_index("xl") * 2 + lax.axis_index("c")).astype(jnp.int32).reshape(1)
    hbm = pl.BlockSpec(memory_space=pltpu.HBM)
    to_key = pl.pallas_call(
        pack_key_kernel,
        out_shape=shape(4, 256, 128),
        in_specs=[hbm] * 2,
        out_specs=vmem()[0],
        scratch_shapes=[pltpu.VMEM((4, 128, 128), BF16)] * 2 + [pltpu.SemaphoreType.DMA((2,))],
        compiler_params=params(61),
        name="pack_key",
    )(keys, values)
    to_query = pl.pallas_call(
        functools.partial(pack_query_kernel, scale),
        out_shape=shape(16, 400, 128),
        in_specs=[pl.BlockSpec(memory_space=pltpu.SMEM)] + [hbm] * 5,
        out_specs=vmem()[0],
        scratch_shapes=[pltpu.VMEM((4, 128, 128), BF16)] * 3
        + [pltpu.VMEM((4, 4, 128), F32), pltpu.VMEM((4, 32, 2048), BF16), pltpu.SemaphoreType.DMA((5,))],
        compiler_params=params(61),
        name="pack_query",
    )(which, queries, out_grad, outputs, logsumexp, bias)
    own = lax.all_to_all(to_key, ("xl", "c"), 0, 0)
    after, before = along(own, -1), along(own, 1)
    k_far, v_far = along(before[:, :128], 1), along(after[:, 128:], -1)
    got_query = lax.all_to_all(to_query, QUERY_GROUP, 0, 0)
    yh = lax.axis_index("yh").astype(jnp.int32).reshape(1)
    dq_parts, own, up, dk_far, dv_far, down, db_parts = pl.pallas_call(
        functools.partial(attend_kernel, scale),
        out_shape=(shape(16, 128, 128),)
        + (shape(4, 256, 128),) * 2
        + (shape(4, 128, 128),) * 2
        + (shape(4, 256, 128), shape(16, 128, 128)),
        in_specs=[pl.BlockSpec(memory_space=pltpu.SMEM)] + vmem(6),
        out_specs=tuple(vmem(7)),
        scratch_shapes=[pltpu.VMEM((512, 512), F32), pltpu.VMEM((512, 512), F32)],
        compiler_params=params(),
        name="attend",
    )(yh, got_query, own, after, k_far, v_far, before)
    up_more, down_more = along(dk_far, 1), along(dv_far, -1)
    up, down = pl.pallas_call(
        fold_kernel,
        out_shape=(shape(4, 256, 128),) * 2,
        in_specs=vmem(4),
        out_specs=tuple(vmem(2)),
        compiler_params=params(),
        name="fold",
    )(up, up_more, down, down_more)
    db = lax.all_to_all(db_parts, ("z", "xh"), 0, 0)
    up, down, db, dq_parts = lax.optimization_barrier((up, down, db, dq_parts))
    up, down = along(up, 1), along(down, -1)
    db = jnp.sum(db.reshape(8, 2, 128, 128).astype(F32), axis=0)
    db = lax.ppermute(db, ("z", "yl"), swaps())
    dq = lax.all_to_all(dq_parts, QUERY_GROUP, 0, 0)
    up, down, db, dq = lax.optimization_barrier((up, down, db, dq))
    joined = pl.pallas_call(
        join_kernel,
        out_shape=shape(4, 384, 128),
        in_specs=vmem(4),
        out_specs=vmem()[0],
        compiler_params=params(),
        name="join",
    )(own, up, down, db)
    joined = lax.all_to_all(joined, ("xl", "c"), 0, 0)
    query_grad = pl.pallas_call(
        unpack_query_kernel,
        out_shape=shape(4, 128, 128),
        in_specs=vmem(1),
        out_specs=vmem()[0],
        compiler_params=params(),
        name="unpack_query",
    )(dq)
    key_grad, value_grad, bias_grad = pl.pallas_call(
        unpack_kernel,
        out_shape=(shape(4, 128, 128),) * 2 + (jax.ShapeDtypeStruct((4, 64, 128), F32),),
        in_specs=vmem(1),
        out_specs=tuple(vmem(3)),
        compiler_params=params(),
        name="unpack",
    )(joined)
    return query_grad, key_grad, value_grad, bias_grad.transpose(0, 2, 1)


def solution(mesh):
    fine = Mesh(mesh.devices.reshape(2, 8, 2, 2, 4, 2), ROW + BLK)
    rows = P(ROW, BLK, None)
    in_specs = (rows, rows, rows, P(None, BLK, None), rows, rows, P(ROW, None, BLK))
    out_specs = (rows, rows, rows, P(None, BLK, ROW))
    return jax.shard_map(body, mesh=fine, in_specs=in_specs, out_specs=out_specs, check_vma=False)
```

```python
import functools

import jax
import jax.numpy as jnp
from jax import lax
from jax.experimental import pallas as pl
from jax.experimental.pallas import tpu as pltpu
from jax.sharding import Mesh
from jax.sharding import PartitionSpec as P

ROW = ("xl", "z", "c")
BLK = ("xh", "yh", "yl")
QUERY_GROUP = ("xl", "c", "xh", "yl")
LOG2E = 1.4426950408889634
AUG = 16
F32, BF16 = jnp.float32, jnp.bfloat16


def two_parts(x):
    high = x.astype(BF16).astype(F32)
    return high, x - high


def fetch(pairs, sems):
    copies = [pltpu.make_async_copy(src, dst, sems.at[at]) for at, (src, dst) in enumerate(pairs)]
    for copy in copies:
        copy.start()
    return copies


def turned(x):
    return x.astype(F32).T.astype(BF16)


def pack_kernel(scale, k_hbm, v_hbm, q_hbm, g_hbm, o_hbm, l_hbm, out_ref, k_ref, v_ref, q_ref, g_ref, o_ref, l_ref, sems):
    copies = fetch(
        ((k_hbm, k_ref), (v_hbm, v_ref), (q_hbm, q_ref), (g_hbm, g_ref), (o_hbm, o_ref), (l_hbm, l_ref)), sems
    )
    lines = lax.broadcasted_iota(jnp.int32, (AUG, 128), 0)
    extra = [jnp.zeros((AUG, 128), F32)] * 4
    for copy in copies[:2]:
        copy.wait()
    for i in range(4):
        k_t, v_t = turned(k_ref[i]), turned(v_ref[i])
        for h in range(4):
            part = slice(h * 32, h * 32 + 32)
            out_ref[h, i * 32 : i * 32 + 32, :] = k_t[part]
            out_ref[h, 128 + i * 32 : 160 + i * 32, :] = v_t[part]
    for copy in copies[2:]:
        copy.wait()
    for i in range(4):
        q_t = turned(q_ref[i])
        g_f = g_ref[i].astype(F32)
        gg = (g_f * o_ref[i].astype(F32)).T
        g_t = g_f.T.astype(BF16)
        for h in range(4):
            part = slice(h * 32, h * 32 + 32)
            offset = l_ref[i, h : h + 1, :] * (-1.0 / scale)
            delta = -jnp.sum(gg[part], axis=0, keepdims=True)
            for at, piece in enumerate(two_parts(offset) + two_parts(delta)):
                extra[h] = jnp.where(lines == i * 4 + at, piece, extra[h])
            out_ref[h, 256 + i * 64 : 288 + i * 64, :] = q_t[part]
            out_ref[h, 288 + i * 64 : 320 + i * 64, :] = g_t[part]
    for h in range(4):
        out_ref[h, 512:528, :] = extra[h].astype(BF16)


def bias_kernel(where_ref, bias_hbm, out_ref, bias_ref, sem):
    copy = pltpu.make_async_copy(bias_hbm.at[where_ref[0]], bias_ref, sem)
    copy.start()
    copy.wait()
    for d in range(4):
        for yh in range(4):
            block = where_ref[1 + d] * 4 + yh
            first = ((block // 8) * 8 + (block % 4) * 2 + (block // 4) % 2) * 128
            out_ref[d, yh * 128 : yh * 128 + 128, :] = bias_ref[:, pl.ds(pl.multiple_of(first, 128), 128)]


def assemble_kernel(got_ref, bias_ref, key_ref, *pay_refs):
    for s in range(4):
        key_ref[s] = got_ref[s, :256, :]
    for d, pay_ref in enumerate(pay_refs):
        for s in range(4):
            pay_ref[s, :272, :] = got_ref[s, 256:528, :]
            pay_ref[s, 272:400, :] = bias_ref[d, s * 128 : s * 128 + 128, :]


def attend_kernel(
    scale,
    where_ref,
    pay0_ref,
    pay1_ref,
    pay2_ref,
    pay3_ref,
    kv0_ref,
    kv1_ref,
    k2_ref,
    v2_ref,
    kv3_ref,
    dq_ref,
    dkv0_ref,
    dkv1_ref,
    dk2_ref,
    dv2_ref,
    dkv3_ref,
    db_ref,
    bias_s,
    acc_s,
):
    dkv_refs = (dkv0_ref, dkv1_ref, None, dkv3_ref)
    owner = [lax.rem(where_ref[5] + p, 4) for p in range(4)]
    pay_refs = (pay0_ref, pay1_ref, pay2_ref, pay3_ref)
    block_of = [where_ref[1 + d] for d in range(4)]
    for d in range(4):
        for p in range(4):
            bias_s[d * 128 : d * 128 + 128, p * 128 : p * 128 + 128] = (
                pay_refs[d][owner[p], 272:400, :].astype(F32) * LOG2E
            )
    acc_s[...] = jnp.zeros_like(acc_s)
    lines = lax.broadcasted_iota(jnp.int32, (AUG, 512), 0)
    ones = [
        jnp.where((lines >= first) & (lines < first + 2), 1.0, 0.0).astype(BF16) for first in range(0, 16, 2)
    ]

    def four_rows(s, carry):
        base = s * 4
        for i in range(4):
            first = i * 64
            q_t, g_t, extra = (
                jnp.concatenate([pay_ref[s, start : start + size, :] for pay_ref in pay_refs], axis=1)
                for start, size in ((first, 32), (first + 32, 32), (256, 16))
            )
            low_at, high_at = slice(i * 32, i * 32 + 32), slice(128 + i * 32, 160 + i * 32)
            k_t = jnp.concatenate(
                [kv0_ref[s, low_at, :], kv1_ref[s, low_at, :], k2_ref[s, low_at, :], kv3_ref[s, low_at, :]], axis=1
            )
            v_t = jnp.concatenate(
                [kv0_ref[s, high_at, :], kv1_ref[s, high_at, :], v2_ref[s, low_at, :], kv3_ref[s, high_at, :]], axis=1
            )
            q_rows = jnp.concatenate([q_t, extra], axis=0).T
            g_rows = jnp.concatenate([g_t, extra], axis=0).T
            k_aug = jnp.concatenate([k_t, ones[i * 2]], axis=0)
            v_aug = jnp.concatenate([v_t, ones[i * 2 + 1]], axis=0)
            scores = jnp.dot(q_rows, k_aug, preferred_element_type=F32)
            prob_grad = jnp.dot(g_rows, v_aug, preferred_element_type=F32)
            probs = jnp.exp2(scores * (scale * LOG2E) + bias_s[...])
            score_grad = probs * prob_grad
            acc_s[...] += score_grad
            low = score_grad.astype(BF16)
            dv = jnp.dot(g_t, probs.astype(BF16), preferred_element_type=F32).astype(BF16)
            dk = (jnp.dot(q_t, low, preferred_element_type=F32) * scale).astype(BF16)
            dq = (jnp.dot(low, k_t.T, preferred_element_type=F32).T * scale).astype(BF16)
            for b in range(4):
                block = slice(b * 128, b * 128 + 128)
                dq_ref[base + block_of[b], i * 32 : i * 32 + 32, :] = dq[:, block]
                if b == 2:
                    dk2_ref[s, low_at, :] = dk[:, block]
                    dv2_ref[s, low_at, :] = dv[:, block]
                else:
                    dkv_refs[b][s, low_at, :] = dk[:, block]
                    dkv_refs[b][s, high_at, :] = dv[:, block]
        return carry

    lax.fori_loop(0, 4, four_rows, 0)
    for p in range(4):
        for d in range(4):
            to = owner[p] * 4 + lax.rem(block_of[d], 2) * 2 + block_of[d] // 2
            db_ref[to] = acc_s[d * 128 : d * 128 + 128, p * 128 : p * 128 + 128].astype(BF16)


def fold_kernel(up_ref, up_more_ref, down_ref, down_more_ref, up_out_ref, down_out_ref):
    for s in range(4):
        up_out_ref[s, :128, :] = (up_ref[s, :128, :].astype(F32) + up_more_ref[s].astype(F32)).astype(BF16)
        up_out_ref[s, 128:, :] = up_ref[s, 128:, :]
        down_out_ref[s, :128, :] = down_ref[s, :128, :]
        down_out_ref[s, 128:, :] = (down_ref[s, 128:, :].astype(F32) + down_more_ref[s].astype(F32)).astype(BF16)


def join_kernel(own_ref, up_ref, down_ref, db_ref, out_ref):
    for s in range(4):
        total = own_ref[s].astype(F32) + up_ref[s].astype(F32) + down_ref[s].astype(F32)
        out_ref[s, :256, :] = total.astype(BF16)
    first_half = lax.broadcasted_iota(jnp.int32, (128, 128), 1) < 64
    for xl in range(2):
        whole = db_ref[xl]
        high = whole.astype(BF16).astype(F32)
        low = whole - high
        out_ref[xl * 2, 256:, :] = jnp.where(first_half, high, pltpu.roll(low, 64, 1)).astype(BF16)
        out_ref[xl * 2 + 1, 256:, :] = jnp.where(first_half, pltpu.roll(high, 64, 1), low).astype(BF16)


def unpack_query_kernel(q_ref, dq_ref):
    for i in range(4):
        heads = []
        for h in range(4):
            parts = [q_ref[h * 4 + a, i * 32 : i * 32 + 32, :].astype(F32) for a in range(4)]
            heads.append(parts[0] + parts[1] + parts[2] + parts[3])
        dq_ref[i] = jnp.concatenate(heads, axis=0).T.astype(BF16)


def unpack_kernel(kv_ref, dk_ref, dv_ref, db_ref):
    for h in range(4):
        parts = kv_ref[h, 256:, :].astype(F32)
        db_ref[h] = (parts + pltpu.roll(parts, 64, 1)).T[:64]
    for i in range(4):
        for first, out in ((0, dk_ref), (128, dv_ref)):
            at = i * 32 + first
            out[i] = turned(jnp.concatenate([kv_ref[h, at : at + 32, :] for h in range(4)], axis=0))


def vmem(n=1):
    return [pl.BlockSpec(memory_space=pltpu.VMEM)] * n


def params(mib=40):
    return pltpu.CompilerParams(vmem_limit_bytes=mib * 2**20)


def swaps():
    return [(z * 2 + yl, ((z // 2) * 2 + yl) * 2 + z % 2) for z in range(8) for yl in range(2)]


def along(value, steps):
    return lax.ppermute(value, "yh", [(n, (n + steps) % 4) for n in range(4)])


def body(queries, keys, values, bias, out_grad, outputs, logsumexp):
    scale = 32 ** (-0.5)
    shape = lambda *s: jax.ShapeDtypeStruct(s, BF16)
    head = lax.axis_index("xl") * 2 + lax.axis_index("c")
    mine = lax.axis_index("xh") * 2 + lax.axis_index("yl")
    where = jnp.stack([head] + [mine ^ d for d in range(4)] + [lax.axis_index("yh")]).astype(jnp.int32)
    hbm = pl.BlockSpec(memory_space=pltpu.HBM)
    smem = pl.BlockSpec(memory_space=pltpu.SMEM)
    packed = pl.pallas_call(
        functools.partial(pack_kernel, scale),
        out_shape=shape(4, 528, 128),
        in_specs=[hbm] * 6,
        out_specs=vmem()[0],
        scratch_shapes=[pltpu.VMEM((4, 128, 128), BF16)] * 5
        + [pltpu.VMEM((4, 4, 128), F32), pltpu.SemaphoreType.DMA((6,))],
        compiler_params=params(61),
        name="pack",
    )(keys, values, queries, out_grad, outputs, logsumexp)
    bias_out = pl.pallas_call(
        bias_kernel,
        out_shape=shape(4, 512, 128),
        in_specs=[smem, hbm],
        out_specs=vmem()[0],
        scratch_shapes=[pltpu.VMEM((128, 2048), BF16), pltpu.SemaphoreType.DMA],
        compiler_params=params(),
        name="bias",
    )(where, bias)
    got = lax.all_to_all(packed, ("xl", "c"), 0, 0)
    own, *pays = pl.pallas_call(
        assemble_kernel,
        out_shape=(shape(4, 256, 128),) + (shape(4, 400, 128),) * 4,
        in_specs=vmem(2),
        out_specs=tuple(vmem(5)),
        compiler_params=params(),
        name="assemble",
    )(got, bias_out)
    after, before = along(own, -1), along(own, 1)
    for d in range(1, 4):
        pays[d] = lax.ppermute(pays[d], ("xh", "yl"), [(n, n ^ d) for n in range(4)])
    k_far, v_far = along(before[:, :128], 1), along(after[:, 128:], -1)
    dq_parts, own, up, dk_far, dv_far, down, db_parts = pl.pallas_call(
        functools.partial(attend_kernel, scale),
        out_shape=(shape(16, 128, 128),)
        + (shape(4, 256, 128),) * 2
        + (shape(4, 128, 128),) * 2
        + (shape(4, 256, 128), shape(16, 128, 128)),
        in_specs=[smem] + vmem(9),
        out_specs=tuple(vmem(7)),
        scratch_shapes=[pltpu.VMEM((512, 512), F32), pltpu.VMEM((512, 512), F32)],
        compiler_params=params(),
        name="attend",
    )(where, *pays, own, after, k_far, v_far, before)
    up_more, down_more = along(dk_far, 1), along(dv_far, -1)
    up, down = pl.pallas_call(
        fold_kernel,
        out_shape=(shape(4, 256, 128),) * 2,
        in_specs=vmem(4),
        out_specs=tuple(vmem(2)),
        compiler_params=params(),
        name="fold",
    )(up, up_more, down, down_more)
    db = lax.all_to_all(db_parts, ("z", "xh"), 0, 0)
    up, down, db, dq_parts = lax.optimization_barrier((up, down, db, dq_parts))
    up, down = along(up, 1), along(down, -1)
    db = jnp.sum(db.reshape(8, 2, 128, 128).astype(F32), axis=0)
    db = lax.ppermute(db, ("z", "yl"), swaps())
    dq = lax.all_to_all(dq_parts, QUERY_GROUP, 0, 0)
    up, down, db, dq = lax.optimization_barrier((up, down, db, dq))
    joined = pl.pallas_call(
        join_kernel,
        out_shape=shape(4, 384, 128),
        in_specs=vmem(4),
        out_specs=vmem()[0],
        compiler_params=params(),
        name="join",
    )(own, up, down, db)
    joined = lax.all_to_all(joined, ("xl", "c"), 0, 0)
    query_grad = pl.pallas_call(
        unpack_query_kernel,
        out_shape=shape(4, 128, 128),
        in_specs=vmem(1),
        out_specs=vmem()[0],
        compiler_params=params(),
        name="unpack_query",
    )(dq)
    key_grad, value_grad, bias_grad = pl.pallas_call(
        unpack_kernel,
        out_shape=(shape(4, 128, 128),) * 2 + (jax.ShapeDtypeStruct((4, 64, 128), F32),),
        in_specs=vmem(1),
        out_specs=tuple(vmem(3)),
        compiler_params=params(),
        name="unpack",
    )(joined)
    return query_grad, key_grad, value_grad, bias_grad.transpose(0, 2, 1)


def solution(mesh):
    fine = Mesh(mesh.devices.reshape(2, 8, 2, 2, 4, 2), ROW + BLK)
    rows = P(ROW, BLK, None)
    in_specs = (rows, rows, rows, P(None, BLK, None), rows, rows, P(ROW, None, BLK))
    out_specs = (rows, rows, rows, P(None, BLK, ROW))
    return jax.shard_map(body, mesh=fine, in_specs=in_specs, out_specs=out_specs, check_vma=False)
```

```python
import functools

import jax
import jax.numpy as jnp
from jax import lax
from jax.experimental import pallas as pl
from jax.experimental.pallas import tpu as pltpu
from jax.sharding import Mesh
from jax.sharding import PartitionSpec as P

ROW = ("xl", "z", "c")
BLK = ("xh", "yh", "yl")
QUERY_GROUP = ("xl", "c", "xh", "yl")
LOG2E = 1.4426950408889634
AUG = 16
F32, BF16 = jnp.float32, jnp.bfloat16


def two_parts(x):
    high = x.astype(BF16).astype(F32)
    return high, x - high


def fetch(pairs, sems):
    copies = [pltpu.make_async_copy(src, dst, sems.at[at]) for at, (src, dst) in enumerate(pairs)]
    for copy in copies:
        copy.start()
    return copies


def turned(x):
    return x.astype(F32).T.astype(BF16)


def pack_kernel(scale, k_hbm, v_hbm, q_hbm, g_hbm, o_hbm, l_hbm, out_ref, k_ref, v_ref, q_ref, g_ref, o_ref, l_ref, sems):
    copies = fetch(
        ((k_hbm, k_ref), (v_hbm, v_ref), (q_hbm, q_ref), (g_hbm, g_ref), (o_hbm, o_ref), (l_hbm, l_ref)), sems
    )
    lines = lax.broadcasted_iota(jnp.int32, (AUG, 128), 0)
    extra = [jnp.zeros((AUG, 128), F32)] * 4
    for copy in copies[:2]:
        copy.wait()
    for i in range(4):
        k_t, v_t = turned(k_ref[i]), turned(v_ref[i])
        for h in range(4):
            part = slice(h * 32, h * 32 + 32)
            out_ref[h, i * 32 : i * 32 + 32, :] = k_t[part]
            out_ref[h, 128 + i * 32 : 160 + i * 32, :] = v_t[part]
    for copy in copies[2:]:
        copy.wait()
    for i in range(4):
        q_t = turned(q_ref[i])
        g_f = g_ref[i].astype(F32)
        gg = (g_f * o_ref[i].astype(F32)).T
        g_t = g_f.T.astype(BF16)
        for h in range(4):
            part = slice(h * 32, h * 32 + 32)
            offset = l_ref[i, h : h + 1, :] * (-1.0 / scale)
            delta = -jnp.sum(gg[part], axis=0, keepdims=True)
            for at, piece in enumerate(two_parts(offset) + two_parts(delta)):
                extra[h] = jnp.where(lines == i * 4 + at, piece, extra[h])
            out_ref[h, 256 + i * 64 : 288 + i * 64, :] = q_t[part]
            out_ref[h, 288 + i * 64 : 320 + i * 64, :] = g_t[part]
    for h in range(4):
        out_ref[h, 512:528, :] = extra[h].astype(BF16)


def bias_kernel(where_ref, bias_hbm, out_ref, bias_ref, sem):
    copy = pltpu.make_async_copy(bias_hbm.at[where_ref[0]], bias_ref, sem)
    copy.start()
    copy.wait()
    for d in range(4):
        for yh in range(4):
            block = where_ref[1 + d] * 4 + yh
            first = ((block // 8) * 8 + (block % 4) * 2 + (block // 4) % 2) * 128
            out_ref[d, yh * 128 : yh * 128 + 128, :] = bias_ref[:, pl.ds(pl.multiple_of(first, 128), 128)]


def assemble_kernel(got_ref, bias_ref, key_ref, *pay_refs):
    for s in range(4):
        key_ref[s] = got_ref[s, :272, :]
    for d, pay_ref in enumerate(pay_refs):
        for s in range(4):
            pay_ref[s, :272, :] = got_ref[s, 256:528, :]
            pay_ref[s, 272:400, :] = bias_ref[d, s * 128 : s * 128 + 128, :]


def attend_kernel(
    scale,
    where_ref,
    pay0_ref,
    pay1_ref,
    pay2_ref,
    pay3_ref,
    kv0_ref,
    kv1_ref,
    k2_ref,
    v2_ref,
    kv3_ref,
    dq_ref,
    dkv0_ref,
    dkv1_ref,
    dk2_ref,
    dv2_ref,
    dkv3_ref,
    db_ref,
    bias_s,
    acc_s,
):
    dkv_refs = (dkv0_ref, dkv1_ref, None, dkv3_ref)
    owner = [lax.rem(where_ref[5] + p, 4) for p in range(4)]
    pay_refs = (pay0_ref, pay1_ref, pay2_ref, pay3_ref)
    block_of = [where_ref[1 + d] for d in range(4)]
    for d in range(4):
        for p in range(4):
            bias_s[d * 128 : d * 128 + 128, p * 128 : p * 128 + 128] = (
                pay_refs[d][owner[p], 272:400, :].astype(F32) * LOG2E
            )
    acc_s[...] = jnp.zeros_like(acc_s)
    lines = lax.broadcasted_iota(jnp.int32, (AUG, 512), 0)
    ones = [
        jnp.where((lines >= first) & (lines < first + 2), 1.0, 0.0).astype(BF16) for first in range(0, 16, 2)
    ]

    def four_rows(s, carry):
        base = s * 4
        for i in range(4):
            first = i * 64
            q_t, g_t, extra = (
                jnp.concatenate([pay_ref[s, start : start + size, :] for pay_ref in pay_refs], axis=1)
                for start, size in ((first, 32), (first + 32, 32), (256, 16))
            )
            low_at, high_at = slice(i * 32, i * 32 + 32), slice(128 + i * 32, 160 + i * 32)
            k_t = jnp.concatenate(
                [kv0_ref[s, low_at, :], kv1_ref[s, low_at, :], k2_ref[s, low_at, :], kv3_ref[s, low_at, :]], axis=1
            )
            v_t = jnp.concatenate(
                [kv0_ref[s, high_at, :], kv1_ref[s, high_at, :], v2_ref[s, low_at, :], kv3_ref[s, high_at, :]], axis=1
            )
            q_rows = jnp.concatenate([q_t, extra], axis=0).T
            g_rows = jnp.concatenate([g_t, extra], axis=0).T
            k_aug = jnp.concatenate([k_t, ones[i * 2]], axis=0)
            v_aug = jnp.concatenate([v_t, ones[i * 2 + 1]], axis=0)
            scores = jnp.dot(q_rows, k_aug, preferred_element_type=F32)
            prob_grad = jnp.dot(g_rows, v_aug, preferred_element_type=F32)
            probs = jnp.exp2(scores * (scale * LOG2E) + bias_s[...])
            score_grad = probs * prob_grad
            acc_s[...] += score_grad
            low = score_grad.astype(BF16)
            dv = jnp.dot(g_t, probs.astype(BF16), preferred_element_type=F32).astype(BF16)
            dk = (jnp.dot(q_t, low, preferred_element_type=F32) * scale).astype(BF16)
            dq = (jnp.dot(low, k_t.T, preferred_element_type=F32).T * scale).astype(BF16)
            for b in range(4):
                block = slice(b * 128, b * 128 + 128)
                dq_ref[base + block_of[b], i * 32 : i * 32 + 32, :] = dq[:, block]
                if b == 2:
                    dk2_ref[s, low_at, :] = dk[:, block]
                    dv2_ref[s, low_at, :] = dv[:, block]
                else:
                    dkv_refs[b][s, low_at, :] = dk[:, block]
                    dkv_refs[b][s, high_at, :] = dv[:, block]
        return carry

    lax.fori_loop(0, 4, four_rows, 0)
    for p in range(4):
        for d in range(4):
            to = owner[p] * 4 + lax.rem(block_of[d], 2) * 2 + block_of[d] // 2
            db_ref[to] = acc_s[d * 128 : d * 128 + 128, p * 128 : p * 128 + 128].astype(BF16)


def fold_kernel(up_ref, up_more_ref, down_ref, down_more_ref, up_out_ref, down_out_ref):
    for s in range(4):
        up_out_ref[s, :128, :] = (up_ref[s, :128, :].astype(F32) + up_more_ref[s].astype(F32)).astype(BF16)
        up_out_ref[s, 128:, :] = up_ref[s, 128:, :]
        down_out_ref[s, :128, :] = down_ref[s, :128, :]
        down_out_ref[s, 128:, :] = (down_ref[s, 128:, :].astype(F32) + down_more_ref[s].astype(F32)).astype(BF16)


def join_kernel(own_ref, up_ref, down_ref, db_ref, out_ref):
    for s in range(4):
        total = own_ref[s].astype(F32) + up_ref[s].astype(F32) + down_ref[s].astype(F32)
        out_ref[s, :256, :] = total.astype(BF16)
    first_half = lax.broadcasted_iota(jnp.int32, (128, 128), 1) < 64
    for xl in range(2):
        whole = db_ref[xl]
        high = whole.astype(BF16).astype(F32)
        low = whole - high
        out_ref[xl * 2, 256:, :] = jnp.where(first_half, high, pltpu.roll(low, 64, 1)).astype(BF16)
        out_ref[xl * 2 + 1, 256:, :] = jnp.where(first_half, pltpu.roll(high, 64, 1), low).astype(BF16)


def unpack_query_kernel(q_ref, dq_ref):
    for i in range(4):
        heads = []
        for h in range(4):
            parts = [q_ref[h * 4 + a, i * 32 : i * 32 + 32, :].astype(F32) for a in range(4)]
            heads.append(parts[0] + parts[1] + parts[2] + parts[3])
        dq_ref[i] = jnp.concatenate(heads, axis=0).T.astype(BF16)


def unpack_kernel(kv_ref, dk_ref, dv_ref, db_ref):
    for h in range(4):
        parts = kv_ref[h, 256:, :].astype(F32)
        db_ref[h] = (parts + pltpu.roll(parts, 64, 1)).T[:64]
    for i in range(4):
        for first, out in ((0, dk_ref), (128, dv_ref)):
            at = i * 32 + first
            out[i] = turned(jnp.concatenate([kv_ref[h, at : at + 32, :] for h in range(4)], axis=0))


def vmem(n=1):
    return [pl.BlockSpec(memory_space=pltpu.VMEM)] * n


def params(mib=40):
    return pltpu.CompilerParams(vmem_limit_bytes=mib * 2**20)


def swaps():
    return [(z * 2 + yl, ((z // 2) * 2 + yl) * 2 + z % 2) for z in range(8) for yl in range(2)]


def along(value, steps):
    return lax.ppermute(value, "yh", [(n, (n + steps) % 4) for n in range(4)])


def body(queries, keys, values, bias, out_grad, outputs, logsumexp):
    scale = 32 ** (-0.5)
    shape = lambda *s: jax.ShapeDtypeStruct(s, BF16)
    head = lax.axis_index("xl") * 2 + lax.axis_index("c")
    mine = lax.axis_index("xh") * 2 + lax.axis_index("yl")
    where = jnp.stack([head] + [mine ^ d for d in range(4)] + [lax.axis_index("yh")]).astype(jnp.int32)
    hbm = pl.BlockSpec(memory_space=pltpu.HBM)
    smem = pl.BlockSpec(memory_space=pltpu.SMEM)
    packed = pl.pallas_call(
        functools.partial(pack_kernel, scale),
        out_shape=shape(4, 528, 128),
        in_specs=[hbm] * 6,
        out_specs=vmem()[0],
        scratch_shapes=[pltpu.VMEM((4, 128, 128), BF16)] * 5
        + [pltpu.VMEM((4, 4, 128), F32), pltpu.SemaphoreType.DMA((6,))],
        compiler_params=params(61),
        name="pack",
    )(keys, values, queries, out_grad, outputs, logsumexp)
    bias_out = pl.pallas_call(
        bias_kernel,
        out_shape=shape(4, 512, 128),
        in_specs=[smem, hbm],
        out_specs=vmem()[0],
        scratch_shapes=[pltpu.VMEM((128, 2048), BF16), pltpu.SemaphoreType.DMA],
        compiler_params=params(),
        name="bias",
    )(where, bias)
    got = lax.all_to_all(packed, ("xl", "c"), 0, 0)
    own, *pays = pl.pallas_call(
        assemble_kernel,
        out_shape=(shape(4, 272, 128),) + (shape(4, 400, 128),) * 4,
        in_specs=vmem(2),
        out_specs=tuple(vmem(5)),
        compiler_params=params(),
        name="assemble",
    )(got, bias_out)
    after, before = along(own, -1), along(own, 1)
    for d in range(1, 4):
        pays[d] = lax.ppermute(pays[d], ("xh", "yl"), [(n, n ^ d) for n in range(4)])
    k_far, v_far = along(before[:, :128], 1), along(after[:, 128:256], -1)
    dq_parts, own, up, dk_far, dv_far, down, db_parts = pl.pallas_call(
        functools.partial(attend_kernel, scale),
        out_shape=(shape(16, 128, 128),)
        + (shape(4, 256, 128),) * 2
        + (shape(4, 128, 128),) * 2
        + (shape(4, 256, 128), shape(16, 128, 128)),
        in_specs=[smem] + vmem(9),
        out_specs=tuple(vmem(7)),
        scratch_shapes=[pltpu.VMEM((512, 512), F32), pltpu.VMEM((512, 512), F32)],
        compiler_params=params(),
        name="attend",
    )(where, *pays, own, after, k_far, v_far, before)
    up_more, down_more = along(dk_far, 1), along(dv_far, -1)
    up, down = pl.pallas_call(
        fold_kernel,
        out_shape=(shape(4, 256, 128),) * 2,
        in_specs=vmem(4),
        out_specs=tuple(vmem(2)),
        compiler_params=params(),
        name="fold",
    )(up, up_more, down, down_more)
    db = lax.all_to_all(db_parts, ("z", "xh"), 0, 0)
    up, down, db, dq_parts = lax.optimization_barrier((up, down, db, dq_parts))
    up, down = along(up, 1), along(down, -1)
    db = jnp.sum(db.reshape(8, 2, 128, 128).astype(F32), axis=0)
    db = lax.ppermute(db, ("z", "yl"), swaps())
    dq = lax.all_to_all(dq_parts, QUERY_GROUP, 0, 0)
    up, down, db, dq = lax.optimization_barrier((up, down, db, dq))
    joined = pl.pallas_call(
        join_kernel,
        out_shape=shape(4, 384, 128),
        in_specs=vmem(4),
        out_specs=vmem()[0],
        compiler_params=params(),
        name="join",
    )(own, up, down, db)
    joined = lax.all_to_all(joined, ("xl", "c"), 0, 0)
    query_grad = pl.pallas_call(
        unpack_query_kernel,
        out_shape=shape(4, 128, 128),
        in_specs=vmem(1),
        out_specs=vmem()[0],
        compiler_params=params(),
        name="unpack_query",
    )(dq)
    key_grad, value_grad, bias_grad = pl.pallas_call(
        unpack_kernel,
        out_shape=(shape(4, 128, 128),) * 2 + (jax.ShapeDtypeStruct((4, 64, 128), F32),),
        in_specs=vmem(1),
        out_specs=tuple(vmem(3)),
        compiler_params=params(),
        name="unpack",
    )(joined)
    return query_grad, key_grad, value_grad, bias_grad.transpose(0, 2, 1)


def solution(mesh):
    fine = Mesh(mesh.devices.reshape(2, 8, 2, 2, 4, 2), ROW + BLK)
    rows = P(ROW, BLK, None)
    in_specs = (rows, rows, rows, P(None, BLK, None), rows, rows, P(ROW, None, BLK))
    out_specs = (rows, rows, rows, P(None, BLK, ROW))
    return jax.shard_map(body, mesh=fine, in_specs=in_specs, out_specs=out_specs, check_vma=False)
```

```python
import functools

import jax
import jax.numpy as jnp
from jax import lax
from jax.experimental import pallas as pl
from jax.experimental.pallas import tpu as pltpu
from jax.sharding import Mesh
from jax.sharding import PartitionSpec as P

ROW = ("xl", "z", "c")
BLK = ("xh", "yh", "yl")
LOG2E = 1.4426950408889634
AUG = 16
F32, BF16 = jnp.float32, jnp.bfloat16


def two_parts(x):
    high = x.astype(BF16).astype(F32)
    return high, x - high


def fetch(pairs, sems):
    copies = [pltpu.make_async_copy(src, dst, sems.at[at]) for at, (src, dst) in enumerate(pairs)]
    for copy in copies:
        copy.start()
    return copies


def turned(x):
    return x.astype(F32).T.astype(BF16)


def pack_kernel(scale, k_hbm, v_hbm, q_hbm, g_hbm, o_hbm, l_hbm, out_ref, k_ref, v_ref, q_ref, g_ref, o_ref, l_ref, sems):
    copies = fetch(
        ((k_hbm, k_ref), (v_hbm, v_ref), (q_hbm, q_ref), (g_hbm, g_ref), (o_hbm, o_ref), (l_hbm, l_ref)), sems
    )
    lines = lax.broadcasted_iota(jnp.int32, (AUG, 128), 0)
    extra = [jnp.zeros((AUG, 128), F32)] * 4
    for copy in copies[:2]:
        copy.wait()
    for i in range(4):
        k_t, v_t = turned(k_ref[i]), turned(v_ref[i])
        for h in range(4):
            part = slice(h * 32, h * 32 + 32)
            out_ref[h, i * 32 : i * 32 + 32, :] = k_t[part]
            out_ref[h, 128 + i * 32 : 160 + i * 32, :] = v_t[part]
    for copy in copies[2:]:
        copy.wait()
    for i in range(4):
        q_t = turned(q_ref[i])
        g_f = g_ref[i].astype(F32)
        gg = (g_f * o_ref[i].astype(F32)).T
        g_t = g_f.T.astype(BF16)
        for h in range(4):
            part = slice(h * 32, h * 32 + 32)
            offset = l_ref[i, h : h + 1, :] * (-1.0 / scale)
            delta = -jnp.sum(gg[part], axis=0, keepdims=True)
            for at, piece in enumerate(two_parts(offset) + two_parts(delta)):
                extra[h] = jnp.where(lines == i * 4 + at, piece, extra[h])
            out_ref[h, 256 + i * 64 : 288 + i * 64, :] = q_t[part]
            out_ref[h, 288 + i * 64 : 320 + i * 64, :] = g_t[part]
    for h in range(4):
        out_ref[h, 512:528, :] = extra[h].astype(BF16)


def bias_kernel(where_ref, bias_hbm, out_ref, bias_ref, sem):
    copy = pltpu.make_async_copy(bias_hbm.at[where_ref[0]], bias_ref, sem)
    copy.start()
    copy.wait()
    for d in range(4):
        for yh in range(4):
            block = where_ref[1 + d] * 4 + yh
            first = ((block // 8) * 8 + (block % 4) * 2 + (block // 4) % 2) * 128
            out_ref[d, yh * 128 : yh * 128 + 128, :] = bias_ref[:, pl.ds(pl.multiple_of(first, 128), 128)]


def assemble_kernel(got_ref, bias_ref, key_ref, *pay_refs):
    for s in range(4):
        key_ref[s] = got_ref[s, :272, :]
    for d, pay_ref in enumerate(pay_refs):
        for s in range(4):
            pay_ref[s, :272, :] = got_ref[s, 256:528, :]
            pay_ref[s, 272:400, :] = bias_ref[d, s * 128 : s * 128 + 128, :]


def attend_kernel(
    scale,
    where_ref,
    pay0_ref,
    pay1_ref,
    pay2_ref,
    pay3_ref,
    kv0_ref,
    kv1_ref,
    k2_ref,
    v2_ref,
    kv3_ref,
    dq0_ref,
    dq1_ref,
    dq2_ref,
    dq3_ref,
    dkv0_ref,
    dkv1_ref,
    dk2_ref,
    dv2_ref,
    dkv3_ref,
    db_ref,
    bias_s,
    acc_s,
):
    dkv_refs = (dkv0_ref, dkv1_ref, None, dkv3_ref)
    owner = [lax.rem(where_ref[5] + p, 4) for p in range(4)]
    dq_refs = (dq0_ref, dq1_ref, dq2_ref, dq3_ref)
    pay_refs = (pay0_ref, pay1_ref, pay2_ref, pay3_ref)
    block_of = [where_ref[1 + d] for d in range(4)]
    for d in range(4):
        for p in range(4):
            bias_s[d * 128 : d * 128 + 128, p * 128 : p * 128 + 128] = (
                pay_refs[d][owner[p], 272:400, :].astype(F32) * LOG2E
            )
    acc_s[...] = jnp.zeros_like(acc_s)
    lines = lax.broadcasted_iota(jnp.int32, (AUG, 512), 0)
    ones = [
        jnp.where((lines >= first) & (lines < first + 2), 1.0, 0.0).astype(BF16) for first in range(0, 16, 2)
    ]

    def four_rows(s, carry):
        for i in range(4):
            first = i * 64
            q_t, g_t, extra = (
                jnp.concatenate([pay_ref[s, start : start + size, :] for pay_ref in pay_refs], axis=1)
                for start, size in ((first, 32), (first + 32, 32), (256, 16))
            )
            low_at, high_at = slice(i * 32, i * 32 + 32), slice(128 + i * 32, 160 + i * 32)
            k_t = jnp.concatenate(
                [kv0_ref[s, low_at, :], kv1_ref[s, low_at, :], k2_ref[s, low_at, :], kv3_ref[s, low_at, :]], axis=1
            )
            v_t = jnp.concatenate(
                [kv0_ref[s, high_at, :], kv1_ref[s, high_at, :], v2_ref[s, low_at, :], kv3_ref[s, high_at, :]], axis=1
            )
            q_rows = jnp.concatenate([q_t, extra], axis=0).T
            g_rows = jnp.concatenate([g_t, extra], axis=0).T
            k_aug = jnp.concatenate([k_t, ones[i * 2]], axis=0)
            v_aug = jnp.concatenate([v_t, ones[i * 2 + 1]], axis=0)
            scores = jnp.dot(q_rows, k_aug, preferred_element_type=F32)
            prob_grad = jnp.dot(g_rows, v_aug, preferred_element_type=F32)
            probs = jnp.exp2(scores * (scale * LOG2E) + bias_s[...])
            score_grad = probs * prob_grad
            acc_s[...] += score_grad
            low = score_grad.astype(BF16)
            dv = jnp.dot(g_t, probs.astype(BF16), preferred_element_type=F32).astype(BF16)
            dk = (jnp.dot(q_t, low, preferred_element_type=F32) * scale).astype(BF16)
            dq = (jnp.dot(low, k_t.T, preferred_element_type=F32).T * scale).astype(BF16)
            for b in range(4):
                block = slice(b * 128, b * 128 + 128)
                dq_refs[b][s, low_at, :] = dq[:, block]
                if b == 2:
                    dk2_ref[s, low_at, :] = dk[:, block]
                    dv2_ref[s, low_at, :] = dv[:, block]
                else:
                    dkv_refs[b][s, low_at, :] = dk[:, block]
                    dkv_refs[b][s, high_at, :] = dv[:, block]
        return carry

    lax.fori_loop(0, 4, four_rows, 0)
    for p in range(4):
        for d in range(4):
            to = owner[p] * 4 + lax.rem(block_of[d], 2) * 2 + block_of[d] // 2
            db_ref[to] = acc_s[d * 128 : d * 128 + 128, p * 128 : p * 128 + 128].astype(BF16)


def fold_kernel(up_ref, up_more_ref, down_ref, down_more_ref, up_out_ref, down_out_ref):
    for s in range(4):
        up_out_ref[s, :128, :] = (up_ref[s, :128, :].astype(F32) + up_more_ref[s].astype(F32)).astype(BF16)
        up_out_ref[s, 128:, :] = up_ref[s, 128:, :]
        down_out_ref[s, :128, :] = down_ref[s, :128, :]
        down_out_ref[s, 128:, :] = (down_ref[s, 128:, :].astype(F32) + down_more_ref[s].astype(F32)).astype(BF16)


def join_kernel(own_ref, up_ref, down_ref, db_ref, dq0_ref, dq1_ref, dq2_ref, dq3_ref, out_ref):
    for s in range(4):
        dq = (dq0_ref[s].astype(F32) + dq1_ref[s].astype(F32)) + (dq2_ref[s].astype(F32) + dq3_ref[s].astype(F32))
        out_ref[s, 384:, :] = dq.astype(BF16)
        total = own_ref[s].astype(F32) + up_ref[s].astype(F32) + down_ref[s].astype(F32)
        out_ref[s, :256, :] = total.astype(BF16)
    first_half = lax.broadcasted_iota(jnp.int32, (128, 128), 1) < 64
    for xl in range(2):
        whole = db_ref[xl]
        high = whole.astype(BF16).astype(F32)
        low = whole - high
        out_ref[xl * 2, 256:384, :] = jnp.where(first_half, high, pltpu.roll(low, 64, 1)).astype(BF16)
        out_ref[xl * 2 + 1, 256:384, :] = jnp.where(first_half, pltpu.roll(high, 64, 1), low).astype(BF16)


def unpack_kernel(got_ref, dq_ref, dk_ref, dv_ref, db_ref):
    for h in range(4):
        parts = got_ref[h, 256:384, :].astype(F32)
        db_ref[h] = (parts + pltpu.roll(parts, 64, 1)).T[:64]
    for i in range(4):
        for first, out in ((0, dk_ref), (128, dv_ref), (384, dq_ref)):
            at = i * 32 + first
            out[i] = turned(jnp.concatenate([got_ref[h, at : at + 32, :] for h in range(4)], axis=0))


def vmem(n=1):
    return [pl.BlockSpec(memory_space=pltpu.VMEM)] * n


def params(mib=40):
    return pltpu.CompilerParams(vmem_limit_bytes=mib * 2**20)


def swaps():
    return [(z * 2 + yl, ((z // 2) * 2 + yl) * 2 + z % 2) for z in range(8) for yl in range(2)]


def along(value, steps):
    return lax.ppermute(value, "yh", [(n, (n + steps) % 4) for n in range(4)])


def body(queries, keys, values, bias, out_grad, outputs, logsumexp):
    scale = 32 ** (-0.5)
    shape = lambda *s: jax.ShapeDtypeStruct(s, BF16)
    head = lax.axis_index("xl") * 2 + lax.axis_index("c")
    mine = lax.axis_index("xh") * 2 + lax.axis_index("yl")
    where = jnp.stack([head] + [mine ^ d for d in range(4)] + [lax.axis_index("yh")]).astype(jnp.int32)
    hbm = pl.BlockSpec(memory_space=pltpu.HBM)
    smem = pl.BlockSpec(memory_space=pltpu.SMEM)
    packed = pl.pallas_call(
        functools.partial(pack_kernel, scale),
        out_shape=shape(4, 528, 128),
        in_specs=[hbm] * 6,
        out_specs=vmem()[0],
        scratch_shapes=[pltpu.VMEM((4, 128, 128), BF16)] * 5
        + [pltpu.VMEM((4, 4, 128), F32), pltpu.SemaphoreType.DMA((6,))],
        compiler_params=params(61),
        name="pack",
    )(keys, values, queries, out_grad, outputs, logsumexp)
    bias_out = pl.pallas_call(
        bias_kernel,
        out_shape=shape(4, 512, 128),
        in_specs=[smem, hbm],
        out_specs=vmem()[0],
        scratch_shapes=[pltpu.VMEM((128, 2048), BF16), pltpu.SemaphoreType.DMA],
        compiler_params=params(),
        name="bias",
    )(where, bias)
    got = lax.all_to_all(packed, ("xl", "c"), 0, 0)
    own, *pays = pl.pallas_call(
        assemble_kernel,
        out_shape=(shape(4, 272, 128),) + (shape(4, 400, 128),) * 4,
        in_specs=vmem(2),
        out_specs=tuple(vmem(5)),
        compiler_params=params(),
        name="assemble",
    )(got, bias_out)
    after, before = along(own, -1), along(own, 1)
    for d in range(1, 4):
        pays[d] = lax.ppermute(pays[d], ("xh", "yl"), [(n, n ^ d) for n in range(4)])
    k_far, v_far = along(before[:, :128], 1), along(after[:, 128:256], -1)
    *dq_parts, own, up, dk_far, dv_far, down, db_parts = pl.pallas_call(
        functools.partial(attend_kernel, scale),
        out_shape=(shape(4, 128, 128),) * 4
        + (shape(4, 256, 128),) * 2
        + (shape(4, 128, 128),) * 2
        + (shape(4, 256, 128), shape(16, 128, 128)),
        in_specs=[smem] + vmem(9),
        out_specs=tuple(vmem(10)),
        scratch_shapes=[pltpu.VMEM((512, 512), F32), pltpu.VMEM((512, 512), F32)],
        compiler_params=params(),
        name="attend",
    )(where, *pays, own, after, k_far, v_far, before)
    up_more, down_more = along(dk_far, 1), along(dv_far, -1)
    up, down = pl.pallas_call(
        fold_kernel,
        out_shape=(shape(4, 256, 128),) * 2,
        in_specs=vmem(4),
        out_specs=tuple(vmem(2)),
        compiler_params=params(),
        name="fold",
    )(up, up_more, down, down_more)
    db = lax.all_to_all(db_parts, ("z", "xh"), 0, 0)
    for d in range(1, 4):
        dq_parts[d] = lax.ppermute(dq_parts[d], ("xh", "yl"), [(n, n ^ d) for n in range(4)])
    up, down, db, dq_parts = lax.optimization_barrier((up, down, db, dq_parts))
    up, down = along(up, 1), along(down, -1)
    db = jnp.sum(db.reshape(8, 2, 128, 128).astype(F32), axis=0)
    db = lax.ppermute(db, ("z", "yl"), swaps())
    joined = pl.pallas_call(
        join_kernel,
        out_shape=shape(4, 512, 128),
        in_specs=vmem(8),
        out_specs=vmem()[0],
        compiler_params=params(),
        name="join",
    )(own, up, down, db, *dq_parts)
    joined = lax.all_to_all(joined, ("xl", "c"), 0, 0)
    query_grad, key_grad, value_grad, bias_grad = pl.pallas_call(
        unpack_kernel,
        out_shape=(shape(4, 128, 128),) * 3 + (jax.ShapeDtypeStruct((4, 64, 128), F32),),
        in_specs=vmem(1),
        out_specs=tuple(vmem(4)),
        compiler_params=params(),
        name="unpack",
    )(joined)
    return query_grad, key_grad, value_grad, bias_grad.transpose(0, 2, 1)


def solution(mesh):
    fine = Mesh(mesh.devices.reshape(2, 8, 2, 2, 4, 2), ROW + BLK)
    rows = P(ROW, BLK, None)
    in_specs = (rows, rows, rows, P(None, BLK, None), rows, rows, P(ROW, None, BLK))
    out_specs = (rows, rows, rows, P(None, BLK, ROW))
    return jax.shard_map(body, mesh=fine, in_specs=in_specs, out_specs=out_specs, check_vma=False)
```

```python
import functools

import jax
import jax.numpy as jnp
from jax import lax
from jax.experimental import pallas as pl
from jax.experimental.pallas import tpu as pltpu
from jax.sharding import Mesh
from jax.sharding import PartitionSpec as P

ROW = ("xl", "z", "c")
BLK = ("xh", "yh", "yl")
LOG2E = 1.4426950408889634
AUG = 16
F32, BF16 = jnp.float32, jnp.bfloat16


def two_parts(x):
    high = x.astype(BF16).astype(F32)
    return high, x - high


def fetch(pairs, sems):
    copies = [pltpu.make_async_copy(src, dst, sems.at[at]) for at, (src, dst) in enumerate(pairs)]
    for copy in copies:
        copy.start()
    return copies


def turned(x):
    return x.astype(F32).T.astype(BF16)


def pack_kernel(scale, k_hbm, v_hbm, q_hbm, g_hbm, o_hbm, l_hbm, out_ref, k_ref, v_ref, q_ref, g_ref, o_ref, l_ref, sems):
    copies = fetch(
        ((k_hbm, k_ref), (v_hbm, v_ref), (q_hbm, q_ref), (g_hbm, g_ref), (o_hbm, o_ref), (l_hbm, l_ref)), sems
    )
    lines = lax.broadcasted_iota(jnp.int32, (AUG, 128), 0)
    extra = [jnp.zeros((AUG, 128), F32)] * 4
    for copy in copies[:2]:
        copy.wait()
    for i in range(4):
        k_t, v_t = turned(k_ref[i]), turned(v_ref[i])
        for h in range(4):
            part = slice(h * 32, h * 32 + 32)
            out_ref[h, i * 32 : i * 32 + 32, :] = k_t[part]
            out_ref[h, 128 + i * 32 : 160 + i * 32, :] = v_t[part]
    for copy in copies[2:]:
        copy.wait()
    for i in range(4):
        q_t = turned(q_ref[i])
        g_f = g_ref[i].astype(F32)
        gg = (g_f * o_ref[i].astype(F32)).T
        g_t = g_f.T.astype(BF16)
        for h in range(4):
            part = slice(h * 32, h * 32 + 32)
            offset = l_ref[i, h : h + 1, :] * (-1.0 / scale)
            delta = -jnp.sum(gg[part], axis=0, keepdims=True)
            for at, piece in enumerate(two_parts(offset) + two_parts(delta)):
                extra[h] = jnp.where(lines == i * 4 + at, piece, extra[h])
            out_ref[h, 256 + i * 64 : 288 + i * 64, :] = q_t[part]
            out_ref[h, 288 + i * 64 : 320 + i * 64, :] = g_t[part]
    for h in range(4):
        out_ref[h, 512:528, :] = extra[h].astype(BF16)


def bias_kernel(where_ref, bias_hbm, out_ref, bias_ref, sem):
    copy = pltpu.make_async_copy(bias_hbm.at[where_ref[0]], bias_ref, sem)
    copy.start()
    copy.wait()
    for d in range(4):
        for yh in range(4):
            block = where_ref[1 + d] * 4 + yh
            first = ((block // 8) * 8 + (block % 4) * 2 + (block // 4) % 2) * 128
            out_ref[d, yh * 128 : yh * 128 + 128, :] = bias_ref[:, pl.ds(pl.multiple_of(first, 128), 128)]


def assemble_kernel(got_ref, bias_ref, key_ref, *pay_refs):
    for s in range(4):
        key_ref[s] = got_ref[s, :272, :]
    for d, pay_ref in enumerate(pay_refs):
        for s in range(4):
            pay_ref[s, :272, :] = got_ref[s, 256:528, :]
            pay_ref[s, 272:400, :] = bias_ref[d, s * 128 : s * 128 + 128, :]


def attend_kernel(
    scale,
    where_ref,
    pay0_ref,
    pay1_ref,
    pay2_ref,
    pay3_ref,
    kv0_ref,
    kv1_ref,
    k2_ref,
    v2_ref,
    kv3_ref,
    dq0_ref,
    dq1_ref,
    dq2_ref,
    dq3_ref,
    dkv0_ref,
    dkv1_ref,
    dk2_ref,
    dv2_ref,
    dkv3_ref,
    db_ref,
    bias_s,
    acc_s,
):
    dkv_refs = (dkv0_ref, dkv1_ref, None, dkv3_ref)
    owner = [lax.rem(where_ref[5] + p, 4) for p in range(4)]
    dq_refs = (dq0_ref, dq1_ref, dq2_ref, dq3_ref)
    pay_refs = (pay0_ref, pay1_ref, pay2_ref, pay3_ref)
    block_of = [where_ref[1 + d] for d in range(4)]
    for d in range(4):
        for p in range(4):
            bias_s[d * 128 : d * 128 + 128, p * 128 : p * 128 + 128] = (
                pay_refs[d][owner[p], 272:400, :].astype(F32) * LOG2E
            )
    acc_s[...] = jnp.zeros_like(acc_s)
    lines = lax.broadcasted_iota(jnp.int32, (AUG, 512), 0)
    ones = [
        jnp.where((lines >= first) & (lines < first + 2), 1.0, 0.0).astype(BF16) for first in range(0, 16, 2)
    ]

    def four_rows(s, carry):
        for i in range(4):
            first = i * 64
            q_t, g_t, extra = (
                jnp.concatenate([pay_ref[s, start : start + size, :] for pay_ref in pay_refs], axis=1)
                for start, size in ((first, 32), (first + 32, 32), (256, 16))
            )
            low_at, high_at = slice(i * 32, i * 32 + 32), slice(128 + i * 32, 160 + i * 32)
            k_t = jnp.concatenate(
                [kv0_ref[s, low_at, :], kv1_ref[s, low_at, :], k2_ref[s, low_at, :], kv3_ref[s, low_at, :]], axis=1
            )
            v_t = jnp.concatenate(
                [kv0_ref[s, high_at, :], kv1_ref[s, high_at, :], v2_ref[s, low_at, :], kv3_ref[s, high_at, :]], axis=1
            )
            q_rows = jnp.concatenate([q_t, extra], axis=0).T
            g_rows = jnp.concatenate([g_t, extra], axis=0).T
            k_aug = jnp.concatenate([k_t, ones[i * 2]], axis=0)
            v_aug = jnp.concatenate([v_t, ones[i * 2 + 1]], axis=0)
            scores = jnp.dot(q_rows, k_aug, preferred_element_type=F32)
            prob_grad = jnp.dot(g_rows, v_aug, preferred_element_type=F32)
            probs = jnp.exp2(scores * (scale * LOG2E) + bias_s[...])
            score_grad = probs * prob_grad
            acc_s[...] += score_grad
            low = score_grad.astype(BF16)
            dv = jnp.dot(g_t, probs.astype(BF16), preferred_element_type=F32).astype(BF16)
            dk = (jnp.dot(q_t, low, preferred_element_type=F32) * scale).astype(BF16)
            dq = (jnp.dot(low, k_t.T, preferred_element_type=F32).T * scale).astype(BF16)
            for b in range(4):
                block = slice(b * 128, b * 128 + 128)
                dq_refs[b][s, low_at, :] = dq[:, block]
                if b == 2:
                    dk2_ref[s, low_at, :] = dk[:, block]
                    dv2_ref[s, low_at, :] = dv[:, block]
                else:
                    dkv_refs[b][s, low_at, :] = dk[:, block]
                    dkv_refs[b][s, high_at, :] = dv[:, block]
        return carry

    lax.fori_loop(0, 4, four_rows, 0)
    for p in range(4):
        for d in range(4):
            to = owner[p] * 4 + lax.rem(block_of[d], 2) * 2 + block_of[d] // 2
            db_ref[to] = acc_s[d * 128 : d * 128 + 128, p * 128 : p * 128 + 128].astype(BF16)


def fold_kernel(up_ref, up_more_ref, down_ref, down_more_ref, up_out_ref, down_out_ref):
    for s in range(4):
        up_out_ref[s, :128, :] = (up_ref[s, :128, :].astype(F32) + up_more_ref[s].astype(F32)).astype(BF16)
        up_out_ref[s, 128:, :] = up_ref[s, 128:, :]
        down_out_ref[s, :128, :] = down_ref[s, :128, :]
        down_out_ref[s, 128:, :] = (down_ref[s, 128:, :].astype(F32) + down_more_ref[s].astype(F32)).astype(BF16)


def join_kernel(own_ref, up_ref, down_ref, db_ref, dq0_ref, dq1_ref, dq2_ref, dq3_ref, out_ref):
    for s in range(4):
        dq = (dq0_ref[s].astype(F32) + dq1_ref[s].astype(F32)) + (dq2_ref[s].astype(F32) + dq3_ref[s].astype(F32))
        out_ref[s, 384:, :] = dq.astype(BF16)
        total = own_ref[s].astype(F32) + up_ref[s].astype(F32) + down_ref[s].astype(F32)
        out_ref[s, :256, :] = total.astype(BF16)
    first_half = lax.broadcasted_iota(jnp.int32, (128, 128), 1) < 64
    for xl in range(2):
        whole = db_ref[xl]
        high = whole.astype(BF16).astype(F32)
        low = whole - high
        out_ref[xl * 2, 256:384, :] = jnp.where(first_half, high, pltpu.roll(low, 64, 1)).astype(BF16)
        out_ref[xl * 2 + 1, 256:384, :] = jnp.where(first_half, pltpu.roll(high, 64, 1), low).astype(BF16)


def unpack_kernel(got_ref, dq_ref, dk_ref, dv_ref, db_ref):
    for h in range(4):
        parts = got_ref[h, 256:384, :].astype(F32)
        db_ref[h] = (parts + pltpu.roll(parts, 64, 1)).T[:64]
    for i in range(4):
        for first, out in ((0, dk_ref), (128, dv_ref), (384, dq_ref)):
            at = i * 32 + first
            out[i] = turned(jnp.concatenate([got_ref[h, at : at + 32, :] for h in range(4)], axis=0))


def vmem(n=1):
    return [pl.BlockSpec(memory_space=pltpu.VMEM)] * n


def params(mib=40):
    return pltpu.CompilerParams(vmem_limit_bytes=mib * 2**20)


def swaps():
    return [(z * 2 + yl, ((z // 2) * 2 + yl) * 2 + z % 2) for z in range(8) for yl in range(2)]


def along(value, steps):
    return lax.ppermute(value, "yh", [(n, (n + steps) % 4) for n in range(4)])


def body(queries, keys, values, bias, out_grad, outputs, logsumexp):
    scale = 32 ** (-0.5)
    shape = lambda *s: jax.ShapeDtypeStruct(s, BF16)
    head = lax.axis_index("xl") * 2 + lax.axis_index("c")
    mine = lax.axis_index("xh") * 2 + lax.axis_index("yl")
    where = jnp.stack([head] + [mine ^ d for d in range(4)] + [lax.axis_index("yh")]).astype(jnp.int32)
    hbm = pl.BlockSpec(memory_space=pltpu.HBM)
    smem = pl.BlockSpec(memory_space=pltpu.SMEM)
    packed = pl.pallas_call(
        functools.partial(pack_kernel, scale),
        out_shape=shape(4, 528, 128),
        in_specs=[hbm] * 6,
        out_specs=vmem()[0],
        scratch_shapes=[pltpu.VMEM((4, 128, 128), BF16)] * 5
        + [pltpu.VMEM((4, 4, 128), F32), pltpu.SemaphoreType.DMA((6,))],
        compiler_params=params(61),
        name="pack",
    )(keys, values, queries, out_grad, outputs, logsumexp)
    bias_out = pl.pallas_call(
        bias_kernel,
        out_shape=shape(4, 512, 128),
        in_specs=[smem, hbm],
        out_specs=vmem()[0],
        scratch_shapes=[pltpu.VMEM((128, 2048), BF16), pltpu.SemaphoreType.DMA],
        compiler_params=params(),
        name="bias",
    )(where, bias)
    got = lax.all_to_all(packed, ("xl", "c"), 0, 0)
    own, *pays = pl.pallas_call(
        assemble_kernel,
        out_shape=(shape(4, 272, 128),) + (shape(4, 400, 128),) * 4,
        in_specs=vmem(2),
        out_specs=tuple(vmem(5)),
        compiler_params=params(),
        name="assemble",
    )(got, bias_out)
    after, before = along(own, -1), along(own, 1)
    for d in range(1, 4):
        pays[d] = lax.ppermute(pays[d], ("xh", "yl"), [(n, n ^ d) for n in range(4)])
    k_far, v_far = along(before[:, :128], 1), along(after[:, 128:256], -1)
    *dq_parts, own, up, dk_far, dv_far, down, db_parts = pl.pallas_call(
        functools.partial(attend_kernel, scale),
        out_shape=(shape(4, 128, 128),) * 4
        + (shape(4, 256, 128),) * 2
        + (shape(4, 128, 128),) * 2
        + (shape(4, 256, 128), shape(16, 128, 128)),
        in_specs=[smem] + vmem(9),
        out_specs=tuple(vmem(10)),
        scratch_shapes=[pltpu.VMEM((512, 512), F32), pltpu.VMEM((512, 512), F32)],
        compiler_params=params(),
        name="attend",
    )(where, *pays, own, after, k_far, v_far, before)
    up_more, down_more = along(dk_far, 1), along(dv_far, -1)
    up, down = pl.pallas_call(
        fold_kernel,
        out_shape=(shape(4, 256, 128),) * 2,
        in_specs=vmem(4),
        out_specs=tuple(vmem(2)),
        compiler_params=params(),
        name="fold",
    )(up, up_more, down, down_more)
    db = lax.all_to_all(db_parts, ("z", "xh"), 0, 0)
    for d in (3,):
        dq_parts[d] = lax.ppermute(dq_parts[d], ("xh", "yl"), [(n, n ^ d) for n in range(4)])
    up, down, db, dq_parts = lax.optimization_barrier((up, down, db, dq_parts))
    for d in (1, 2):
        dq_parts[d] = lax.ppermute(dq_parts[d], ("xh", "yl"), [(n, n ^ d) for n in range(4)])
    up, down = along(up, 1), along(down, -1)
    db = jnp.sum(db.reshape(8, 2, 128, 128).astype(F32), axis=0)
    db = lax.ppermute(db, ("z", "yl"), swaps())
    joined = pl.pallas_call(
        join_kernel,
        out_shape=shape(4, 512, 128),
        in_specs=vmem(8),
        out_specs=vmem()[0],
        compiler_params=params(),
        name="join",
    )(own, up, down, db, *dq_parts)
    joined = lax.all_to_all(joined, ("xl", "c"), 0, 0)
    query_grad, key_grad, value_grad, bias_grad = pl.pallas_call(
        unpack_kernel,
        out_shape=(shape(4, 128, 128),) * 3 + (jax.ShapeDtypeStruct((4, 64, 128), F32),),
        in_specs=vmem(1),
        out_specs=tuple(vmem(4)),
        compiler_params=params(),
        name="unpack",
    )(joined)
    return query_grad, key_grad, value_grad, bias_grad.transpose(0, 2, 1)


def solution(mesh):
    fine = Mesh(mesh.devices.reshape(2, 8, 2, 2, 4, 2), ROW + BLK)
    rows = P(ROW, BLK, None)
    in_specs = (rows, rows, rows, P(None, BLK, None), rows, rows, P(ROW, None, BLK))
    out_specs = (rows, rows, rows, P(None, BLK, ROW))
    return jax.shard_map(body, mesh=fine, in_specs=in_specs, out_specs=out_specs, check_vma=False)
```

```python
import functools

import jax
import jax.numpy as jnp
from jax import lax
from jax.experimental import pallas as pl
from jax.experimental.pallas import tpu as pltpu
from jax.sharding import Mesh
from jax.sharding import PartitionSpec as P

ROW = ("xl", "z", "c")
BLK = ("xh", "yh", "yl")
LOG2E = 1.4426950408889634
AUG = 16
FLIPS = (0, 3, 2, 1)
F32, BF16 = jnp.float32, jnp.bfloat16


def two_parts(x):
    high = x.astype(BF16).astype(F32)
    return high, x - high


def fetch(pairs, sems):
    copies = [pltpu.make_async_copy(src, dst, sems.at[at]) for at, (src, dst) in enumerate(pairs)]
    for copy in copies:
        copy.start()
    return copies


def turned(x):
    return x.astype(F32).T.astype(BF16)


def pack_kernel(scale, k_hbm, v_hbm, q_hbm, g_hbm, o_hbm, l_hbm, out_ref, k_ref, v_ref, q_ref, g_ref, o_ref, l_ref, sems):
    copies = fetch(
        ((k_hbm, k_ref), (v_hbm, v_ref), (q_hbm, q_ref), (g_hbm, g_ref), (o_hbm, o_ref), (l_hbm, l_ref)), sems
    )
    lines = lax.broadcasted_iota(jnp.int32, (AUG, 128), 0)
    extra = [jnp.zeros((AUG, 128), F32)] * 4
    for copy in copies[:2]:
        copy.wait()
    for i in range(4):
        k_t, v_t = turned(k_ref[i]), turned(v_ref[i])
        for h in range(4):
            part = slice(h * 32, h * 32 + 32)
            out_ref[h, i * 32 : i * 32 + 32, :] = k_t[part]
            out_ref[h, 128 + i * 32 : 160 + i * 32, :] = v_t[part]
    for copy in copies[2:]:
        copy.wait()
    for i in range(4):
        q_t = turned(q_ref[i])
        g_f = g_ref[i].astype(F32)
        gg = (g_f * o_ref[i].astype(F32)).T
        g_t = g_f.T.astype(BF16)
        for h in range(4):
            part = slice(h * 32, h * 32 + 32)
            offset = l_ref[i, h : h + 1, :] * (-1.0 / scale)
            delta = -jnp.sum(gg[part], axis=0, keepdims=True)
            for at, piece in enumerate(two_parts(offset) + two_parts(delta)):
                extra[h] = jnp.where(lines == i * 4 + at, piece, extra[h])
            out_ref[h, 256 + i * 64 : 288 + i * 64, :] = q_t[part]
            out_ref[h, 288 + i * 64 : 320 + i * 64, :] = g_t[part]
    for h in range(4):
        out_ref[h, 512:528, :] = extra[h].astype(BF16)


def bias_kernel(where_ref, bias_hbm, out_ref, bias_ref, sem):
    copy = pltpu.make_async_copy(bias_hbm.at[where_ref[0]], bias_ref, sem)
    copy.start()
    copy.wait()
    for d in range(4):
        for yh in range(4):
            block = where_ref[1 + d] * 4 + yh
            first = ((block // 8) * 8 + (block % 4) * 2 + (block // 4) % 2) * 128
            out_ref[d, yh * 128 : yh * 128 + 128, :] = bias_ref[:, pl.ds(pl.multiple_of(first, 128), 128)]


def assemble_kernel(got_ref, bias_ref, key_ref, *pay_refs):
    for s in range(4):
        key_ref[s] = got_ref[s, :272, :]
    for d, pay_ref in enumerate(pay_refs):
        for s in range(4):
            pay_ref[s, :272, :] = got_ref[s, 256:528, :]
            pay_ref[s, 272:400, :] = bias_ref[d, s * 128 : s * 128 + 128, :]


def attend_kernel(
    scale,
    where_ref,
    pay0_ref,
    pay1_ref,
    pay2_ref,
    pay3_ref,
    kv0_ref,
    kv1_ref,
    k2_ref,
    v2_ref,
    kv3_ref,
    dq0_ref,
    dq1_ref,
    dq2_ref,
    dq3_ref,
    dkv0_ref,
    dkv1_ref,
    dk2_ref,
    dv2_ref,
    dkv3_ref,
    db_ref,
    bias_s,
    acc_s,
):
    dkv_refs = (dkv0_ref, dkv1_ref, None, dkv3_ref)
    owner = [lax.rem(where_ref[5] + p, 4) for p in range(4)]
    dq_refs = (dq0_ref, dq1_ref, dq2_ref, dq3_ref)
    pay_refs = (pay0_ref, pay1_ref, pay2_ref, pay3_ref)
    block_of = [where_ref[1 + d] for d in range(4)]
    for d in range(4):
        for p in range(4):
            bias_s[d * 128 : d * 128 + 128, p * 128 : p * 128 + 128] = (
                pay_refs[d][owner[p], 272:400, :].astype(F32) * LOG2E
            )
    acc_s[...] = jnp.zeros_like(acc_s)
    lines = lax.broadcasted_iota(jnp.int32, (AUG, 512), 0)
    ones = [
        jnp.where((lines >= first) & (lines < first + 2), 1.0, 0.0).astype(BF16) for first in range(0, 16, 2)
    ]

    def four_rows(s, carry):
        for i in range(4):
            first = i * 64
            q_t, g_t, extra = (
                jnp.concatenate([pay_ref[s, start : start + size, :] for pay_ref in pay_refs], axis=1)
                for start, size in ((first, 32), (first + 32, 32), (256, 16))
            )
            low_at, high_at = slice(i * 32, i * 32 + 32), slice(128 + i * 32, 160 + i * 32)
            k_t = jnp.concatenate(
                [kv0_ref[s, low_at, :], kv1_ref[s, low_at, :], k2_ref[s, low_at, :], kv3_ref[s, low_at, :]], axis=1
            )
            v_t = jnp.concatenate(
                [kv0_ref[s, high_at, :], kv1_ref[s, high_at, :], v2_ref[s, low_at, :], kv3_ref[s, high_at, :]], axis=1
            )
            q_rows = jnp.concatenate([q_t, extra], axis=0).T
            g_rows = jnp.concatenate([g_t, extra], axis=0).T
            k_aug = jnp.concatenate([k_t, ones[i * 2]], axis=0)
            v_aug = jnp.concatenate([v_t, ones[i * 2 + 1]], axis=0)
            scores = jnp.dot(q_rows, k_aug, preferred_element_type=F32)
            prob_grad = jnp.dot(g_rows, v_aug, preferred_element_type=F32)
            probs = jnp.exp2(scores * (scale * LOG2E) + bias_s[...])
            score_grad = probs * prob_grad
            acc_s[...] += score_grad
            low = score_grad.astype(BF16)
            dv = jnp.dot(g_t, probs.astype(BF16), preferred_element_type=F32).astype(BF16)
            dk = (jnp.dot(q_t, low, preferred_element_type=F32) * scale).astype(BF16)
            dq = (jnp.dot(low, k_t.T, preferred_element_type=F32).T * scale).astype(BF16)
            for b in range(4):
                block = slice(b * 128, b * 128 + 128)
                dq_refs[b][s, low_at, :] = dq[:, block]
                if b == 2:
                    dk2_ref[s, low_at, :] = dk[:, block]
                    dv2_ref[s, low_at, :] = dv[:, block]
                else:
                    dkv_refs[b][s, low_at, :] = dk[:, block]
                    dkv_refs[b][s, high_at, :] = dv[:, block]
        return carry

    lax.fori_loop(0, 4, four_rows, 0)
    for p in range(4):
        for d in range(4):
            to = owner[p] * 4 + lax.rem(block_of[d], 2) * 2 + block_of[d] // 2
            db_ref[to] = acc_s[d * 128 : d * 128 + 128, p * 128 : p * 128 + 128].astype(BF16)


def fold_kernel(up_ref, up_more_ref, down_ref, down_more_ref, up_out_ref, down_out_ref):
    for s in range(4):
        up_out_ref[s, :128, :] = (up_ref[s, :128, :].astype(F32) + up_more_ref[s].astype(F32)).astype(BF16)
        up_out_ref[s, 128:, :] = up_ref[s, 128:, :]
        down_out_ref[s, :128, :] = down_ref[s, :128, :]
        down_out_ref[s, 128:, :] = (down_ref[s, 128:, :].astype(F32) + down_more_ref[s].astype(F32)).astype(BF16)


def join_kernel(own_ref, up_ref, down_ref, db_ref, dq0_ref, dq1_ref, dq2_ref, dq3_ref, out_ref):
    for s in range(4):
        dq = (dq0_ref[s].astype(F32) + dq1_ref[s].astype(F32)) + (dq2_ref[s].astype(F32) + dq3_ref[s].astype(F32))
        out_ref[s, 384:, :] = dq.astype(BF16)
        total = own_ref[s].astype(F32) + up_ref[s].astype(F32) + down_ref[s].astype(F32)
        out_ref[s, :256, :] = total.astype(BF16)
    first_half = lax.broadcasted_iota(jnp.int32, (128, 128), 1) < 64
    for xl in range(2):
        whole = db_ref[xl]
        high = whole.astype(BF16).astype(F32)
        low = whole - high
        out_ref[xl * 2, 256:384, :] = jnp.where(first_half, high, pltpu.roll(low, 64, 1)).astype(BF16)
        out_ref[xl * 2 + 1, 256:384, :] = jnp.where(first_half, pltpu.roll(high, 64, 1), low).astype(BF16)


def unpack_kernel(got_ref, dq_ref, dk_ref, dv_ref, db_ref):
    for h in range(4):
        parts = got_ref[h, 256:384, :].astype(F32)
        db_ref[h] = (parts + pltpu.roll(parts, 64, 1)).T[:64]
    for i in range(4):
        for first, out in ((0, dk_ref), (128, dv_ref), (384, dq_ref)):
            at = i * 32 + first
            out[i] = turned(jnp.concatenate([got_ref[h, at : at + 32, :] for h in range(4)], axis=0))


def vmem(n=1):
    return [pl.BlockSpec(memory_space=pltpu.VMEM)] * n


def params(mib=40):
    return pltpu.CompilerParams(vmem_limit_bytes=mib * 2**20)


def swaps():
    return [(z * 2 + yl, ((z // 2) * 2 + yl) * 2 + z % 2) for z in range(8) for yl in range(2)]


def along(value, steps):
    return lax.ppermute(value, "yh", [(n, (n + steps) % 4) for n in range(4)])


def body(queries, keys, values, bias, out_grad, outputs, logsumexp):
    scale = 32 ** (-0.5)
    shape = lambda *s: jax.ShapeDtypeStruct(s, BF16)
    head = lax.axis_index("xl") * 2 + lax.axis_index("c")
    mine = lax.axis_index("xh") * 2 + lax.axis_index("yl")
    where = jnp.stack([head] + [mine ^ d for d in FLIPS] + [lax.axis_index("yh")]).astype(jnp.int32)
    hbm = pl.BlockSpec(memory_space=pltpu.HBM)
    smem = pl.BlockSpec(memory_space=pltpu.SMEM)
    packed = pl.pallas_call(
        functools.partial(pack_kernel, scale),
        out_shape=shape(4, 528, 128),
        in_specs=[hbm] * 6,
        out_specs=vmem()[0],
        scratch_shapes=[pltpu.VMEM((4, 128, 128), BF16)] * 5
        + [pltpu.VMEM((4, 4, 128), F32), pltpu.SemaphoreType.DMA((6,))],
        compiler_params=params(61),
        name="pack",
    )(keys, values, queries, out_grad, outputs, logsumexp)
    bias_out = pl.pallas_call(
        bias_kernel,
        out_shape=shape(4, 512, 128),
        in_specs=[smem, hbm],
        out_specs=vmem()[0],
        scratch_shapes=[pltpu.VMEM((128, 2048), BF16), pltpu.SemaphoreType.DMA],
        compiler_params=params(),
        name="bias",
    )(where, bias)
    got = lax.all_to_all(packed, ("xl", "c"), 0, 0)
    own, *pays = pl.pallas_call(
        assemble_kernel,
        out_shape=(shape(4, 272, 128),) + (shape(4, 400, 128),) * 4,
        in_specs=vmem(2),
        out_specs=tuple(vmem(5)),
        compiler_params=params(),
        name="assemble",
    )(got, bias_out)
    after, before = along(own, -1), along(own, 1)
    for d in range(1, 4):
        pays[d] = lax.ppermute(pays[d], ("xh", "yl"), [(n, n ^ FLIPS[d]) for n in range(4)])
    k_far, v_far = along(before[:, :128], 1), along(after[:, 128:256], -1)
    *dq_parts, own, up, dk_far, dv_far, down, db_parts = pl.pallas_call(
        functools.partial(attend_kernel, scale),
        out_shape=(shape(4, 128, 128),) * 4
        + (shape(4, 256, 128),) * 2
        + (shape(4, 128, 128),) * 2
        + (shape(4, 256, 128), shape(16, 128, 128)),
        in_specs=[smem] + vmem(9),
        out_specs=tuple(vmem(10)),
        scratch_shapes=[pltpu.VMEM((512, 512), F32), pltpu.VMEM((512, 512), F32)],
        compiler_params=params(),
        name="attend",
    )(where, *pays, own, after, k_far, v_far, before)
    up_more, down_more = along(dk_far, 1), along(dv_far, -1)
    up, down = pl.pallas_call(
        fold_kernel,
        out_shape=(shape(4, 256, 128),) * 2,
        in_specs=vmem(4),
        out_specs=tuple(vmem(2)),
        compiler_params=params(),
        name="fold",
    )(up, up_more, down, down_more)
    db = lax.all_to_all(db_parts, ("z", "xh"), 0, 0)
    up, down, db, dq_parts = lax.optimization_barrier((up, down, db, dq_parts))
    for d in range(1, 4):
        dq_parts[d] = lax.ppermute(dq_parts[d], ("xh", "yl"), [(n, n ^ FLIPS[d]) for n in range(4)])
    up, down = along(up, 1), along(down, -1)
    db = jnp.sum(db.reshape(8, 2, 128, 128).astype(F32), axis=0)
    db = lax.ppermute(db, ("z", "yl"), swaps())
    joined = pl.pallas_call(
        join_kernel,
        out_shape=shape(4, 512, 128),
        in_specs=vmem(8),
        out_specs=vmem()[0],
        compiler_params=params(),
        name="join",
    )(own, up, down, db, *dq_parts)
    joined = lax.all_to_all(joined, ("xl", "c"), 0, 0)
    query_grad, key_grad, value_grad, bias_grad = pl.pallas_call(
        unpack_kernel,
        out_shape=(shape(4, 128, 128),) * 3 + (jax.ShapeDtypeStruct((4, 64, 128), F32),),
        in_specs=vmem(1),
        out_specs=tuple(vmem(4)),
        compiler_params=params(),
        name="unpack",
    )(joined)
    return query_grad, key_grad, value_grad, bias_grad.transpose(0, 2, 1)


def solution(mesh):
    fine = Mesh(mesh.devices.reshape(2, 8, 2, 2, 4, 2), ROW + BLK)
    rows = P(ROW, BLK, None)
    in_specs = (rows, rows, rows, P(None, BLK, None), rows, rows, P(ROW, None, BLK))
    out_specs = (rows, rows, rows, P(None, BLK, ROW))
    return jax.shard_map(body, mesh=fine, in_specs=in_specs, out_specs=out_specs, check_vma=False)
```

```python
import functools

import jax
import jax.numpy as jnp
from jax import lax
from jax.experimental import pallas as pl
from jax.experimental.pallas import tpu as pltpu
from jax.sharding import Mesh
from jax.sharding import PartitionSpec as P

ROW = ("xl", "z", "c")
BLK = ("xh", "yh", "yl")
LOG2E = 1.4426950408889634
AUG = 16
FLIPS = (0, 3, 2, 1)
F32, BF16 = jnp.float32, jnp.bfloat16


def two_parts(x):
    high = x.astype(BF16).astype(F32)
    return high, x - high


def fetch(pairs, sems):
    copies = [pltpu.make_async_copy(src, dst, sems.at[at]) for at, (src, dst) in enumerate(pairs)]
    for copy in copies:
        copy.start()
    return copies


def turned(x):
    return x.astype(F32).T.astype(BF16)


def pack_kernel(scale, k_hbm, v_hbm, q_hbm, g_hbm, o_hbm, l_hbm, out_ref, k_ref, v_ref, q_ref, g_ref, o_ref, l_ref, sems):
    copies = fetch(
        ((k_hbm, k_ref), (v_hbm, v_ref), (q_hbm, q_ref), (g_hbm, g_ref), (o_hbm, o_ref), (l_hbm, l_ref)), sems
    )
    lines = lax.broadcasted_iota(jnp.int32, (AUG, 128), 0)
    extra = [jnp.zeros((AUG, 128), F32)] * 4
    for copy in copies[:2]:
        copy.wait()
    for i in range(4):
        k_t, v_t = turned(k_ref[i]), turned(v_ref[i])
        for h in range(4):
            part = slice(h * 32, h * 32 + 32)
            out_ref[h, i * 32 : i * 32 + 32, :] = k_t[part]
            out_ref[h, 128 + i * 32 : 160 + i * 32, :] = v_t[part]
    for copy in copies[2:]:
        copy.wait()
    for i in range(4):
        q_t = turned(q_ref[i])
        g_f = g_ref[i].astype(F32)
        gg = (g_f * o_ref[i].astype(F32)).T
        g_t = g_f.T.astype(BF16)
        for h in range(4):
            part = slice(h * 32, h * 32 + 32)
            offset = l_ref[i, h : h + 1, :] * (-1.0 / scale)
            delta = -jnp.sum(gg[part], axis=0, keepdims=True)
            for at, piece in enumerate(two_parts(offset) + two_parts(delta)):
                extra[h] = jnp.where(lines == i * 4 + at, piece, extra[h])
            out_ref[h, 256 + i * 64 : 288 + i * 64, :] = q_t[part]
            out_ref[h, 288 + i * 64 : 320 + i * 64, :] = g_t[part]
    for h in range(4):
        out_ref[h, 512:528, :] = extra[h].astype(BF16)


def bias_kernel(where_ref, bias_hbm, out_ref, bias_ref, sem):
    copy = pltpu.make_async_copy(bias_hbm.at[where_ref[0]], bias_ref, sem)
    copy.start()
    copy.wait()
    for d in range(4):
        for yh in range(4):
            block = where_ref[1 + d] * 4 + yh
            first = ((block // 8) * 8 + (block % 4) * 2 + (block // 4) % 2) * 128
            out_ref[d, yh * 128 : yh * 128 + 128, :] = bias_ref[:, pl.ds(pl.multiple_of(first, 128), 128)]


def assemble_kernel(got_ref, bias_ref, key_ref, *pay_refs):
    for s in range(4):
        key_ref[s] = got_ref[s, :272, :]
    for d, pay_ref in enumerate(pay_refs):
        for s in range(4):
            pay_ref[s, :272, :] = got_ref[s, 256:528, :]
            pay_ref[s, 272:400, :] = bias_ref[d, s * 128 : s * 128 + 128, :]


def attend_kernel(
    scale,
    where_ref,
    pay0_ref,
    pay1_ref,
    pay2_ref,
    pay3_ref,
    kv0_ref,
    kv1_ref,
    k2_ref,
    v2_ref,
    kv3_ref,
    dq0_ref,
    dq1_ref,
    dq2_ref,
    dq3_ref,
    dkv0_ref,
    dkv1_ref,
    dk2_ref,
    dv2_ref,
    dkv3_ref,
    db_ref,
    bias_s,
    acc_s,
):
    dkv_refs = (dkv0_ref, dkv1_ref, None, dkv3_ref)
    owner = [lax.rem(where_ref[5] + p, 4) for p in range(4)]
    dq_refs = (dq0_ref, dq1_ref, dq2_ref, dq3_ref)
    pay_refs = (pay0_ref, pay1_ref, pay2_ref, pay3_ref)
    block_of = [where_ref[1 + d] for d in range(4)]
    for d in range(4):
        for p in range(4):
            bias_s[d * 128 : d * 128 + 128, p * 128 : p * 128 + 128] = (
                pay_refs[d][owner[p], 272:400, :].astype(F32) * LOG2E
            )
    acc_s[...] = jnp.zeros_like(acc_s)
    lines = lax.broadcasted_iota(jnp.int32, (AUG, 512), 0)
    ones = [
        jnp.where((lines >= first) & (lines < first + 2), 1.0, 0.0).astype(BF16) for first in range(0, 16, 2)
    ]

    def four_rows(s, carry):
        for i in range(4):
            first = i * 64
            q_t, g_t, extra = (
                jnp.concatenate([pay_ref[s, start : start + size, :] for pay_ref in pay_refs], axis=1)
                for start, size in ((first, 32), (first + 32, 32), (256, 16))
            )
            low_at, high_at = slice(i * 32, i * 32 + 32), slice(128 + i * 32, 160 + i * 32)
            k_t = jnp.concatenate(
                [kv0_ref[s, low_at, :], kv1_ref[s, low_at, :], k2_ref[s, low_at, :], kv3_ref[s, low_at, :]], axis=1
            )
            v_t = jnp.concatenate(
                [kv0_ref[s, high_at, :], kv1_ref[s, high_at, :], v2_ref[s, low_at, :], kv3_ref[s, high_at, :]], axis=1
            )
            q_rows = jnp.concatenate([q_t, extra], axis=0).T
            g_rows = jnp.concatenate([g_t, extra], axis=0).T
            k_aug = jnp.concatenate([k_t, ones[i * 2]], axis=0)
            v_aug = jnp.concatenate([v_t, ones[i * 2 + 1]], axis=0)
            scores = jnp.dot(q_rows, k_aug, preferred_element_type=F32)
            prob_grad = jnp.dot(g_rows, v_aug, preferred_element_type=F32)
            probs = jnp.exp2(scores * (scale * LOG2E) + bias_s[...])
            score_grad = probs * prob_grad
            acc_s[...] += score_grad
            low = score_grad.astype(BF16)
            dv = jnp.dot(g_t, probs.astype(BF16), preferred_element_type=F32).astype(BF16)
            dk = (jnp.dot(q_t, low, preferred_element_type=F32) * scale).astype(BF16)
            dq = (jnp.dot(low, k_t.T, preferred_element_type=F32).T * scale).astype(BF16)
            for b in range(4):
                block = slice(b * 128, b * 128 + 128)
                dq_refs[b][s, low_at, :] = dq[:, block]
                if b == 2:
                    dk2_ref[s, low_at, :] = dk[:, block]
                    dv2_ref[s, low_at, :] = dv[:, block]
                else:
                    dkv_refs[b][s, low_at, :] = dk[:, block]
                    dkv_refs[b][s, high_at, :] = dv[:, block]
        return carry

    lax.fori_loop(0, 4, four_rows, 0)
    for p in range(4):
        for d in range(4):
            to = owner[p] * 4 + lax.rem(block_of[d], 2) * 2 + block_of[d] // 2
            db_ref[to] = acc_s[d * 128 : d * 128 + 128, p * 128 : p * 128 + 128].astype(BF16)


def fold_kernel(up_ref, up_more_ref, down_ref, down_more_ref, up_out_ref, down_out_ref):
    for s in range(4):
        up_out_ref[s, :128, :] = (up_ref[s, :128, :].astype(F32) + up_more_ref[s].astype(F32)).astype(BF16)
        up_out_ref[s, 128:, :] = up_ref[s, 128:, :]
        down_out_ref[s, :128, :] = down_ref[s, :128, :]
        down_out_ref[s, 128:, :] = (down_ref[s, 128:, :].astype(F32) + down_more_ref[s].astype(F32)).astype(BF16)


def join_kernel(own_ref, up_ref, down_ref, db_ref, dq0_ref, dq1_ref, dq2_ref, dq3_ref, out_ref):
    for s in range(4):
        dq = (dq0_ref[s].astype(F32) + dq1_ref[s].astype(F32)) + (dq2_ref[s].astype(F32) + dq3_ref[s].astype(F32))
        out_ref[s, 384:, :] = dq.astype(BF16)
        total = own_ref[s].astype(F32) + up_ref[s].astype(F32) + down_ref[s].astype(F32)
        out_ref[s, :256, :] = total.astype(BF16)
    first_half = lax.broadcasted_iota(jnp.int32, (128, 128), 1) < 64
    for xl in range(2):
        whole = db_ref[xl]
        high = whole.astype(BF16).astype(F32)
        low = whole - high
        out_ref[xl * 2, 256:384, :] = jnp.where(first_half, high, pltpu.roll(low, 64, 1)).astype(BF16)
        out_ref[xl * 2 + 1, 256:384, :] = jnp.where(first_half, pltpu.roll(high, 64, 1), low).astype(BF16)


def unpack_kernel(got_ref, dq_ref, dk_ref, dv_ref, db_ref):
    for h in range(4):
        parts = got_ref[h, 256:384, :].astype(F32)
        db_ref[h] = (parts + pltpu.roll(parts, 64, 1)).T[:64]
    for i in range(4):
        for first, out in ((0, dk_ref), (128, dv_ref), (384, dq_ref)):
            at = i * 32 + first
            out[i] = turned(jnp.concatenate([got_ref[h, at : at + 32, :] for h in range(4)], axis=0))


def vmem(n=1):
    return [pl.BlockSpec(memory_space=pltpu.VMEM)] * n


def params(mib=40):
    return pltpu.CompilerParams(vmem_limit_bytes=mib * 2**20)


def swaps():
    return [(z * 2 + yl, ((z // 2) * 2 + yl) * 2 + z % 2) for z in range(8) for yl in range(2)]


def along(value, steps):
    return lax.ppermute(value, "yh", [(n, (n + steps) % 4) for n in range(4)])


def body(queries, keys, values, bias, out_grad, outputs, logsumexp):
    scale = 32 ** (-0.5)
    shape = lambda *s: jax.ShapeDtypeStruct(s, BF16)
    head = lax.axis_index("xl") * 2 + lax.axis_index("c")
    mine = lax.axis_index("xh") * 2 + lax.axis_index("yl")
    where = jnp.stack([head] + [mine ^ d for d in FLIPS] + [lax.axis_index("yh")]).astype(jnp.int32)
    hbm = pl.BlockSpec(memory_space=pltpu.HBM)
    smem = pl.BlockSpec(memory_space=pltpu.SMEM)
    packed = pl.pallas_call(
        functools.partial(pack_kernel, scale),
        out_shape=shape(4, 528, 128),
        in_specs=[hbm] * 6,
        out_specs=vmem()[0],
        scratch_shapes=[pltpu.VMEM((4, 128, 128), BF16)] * 5
        + [pltpu.VMEM((4, 4, 128), F32), pltpu.SemaphoreType.DMA((6,))],
        compiler_params=params(61),
        name="pack",
    )(keys, values, queries, out_grad, outputs, logsumexp)
    bias_out = pl.pallas_call(
        bias_kernel,
        out_shape=shape(4, 512, 128),
        in_specs=[smem, hbm],
        out_specs=vmem()[0],
        scratch_shapes=[pltpu.VMEM((128, 2048), BF16), pltpu.SemaphoreType.DMA],
        compiler_params=params(),
        name="bias",
    )(where, bias)
    got = lax.all_to_all(packed, ("xl", "c"), 0, 0)
    own, *pays = pl.pallas_call(
        assemble_kernel,
        out_shape=(shape(4, 272, 128),) + (shape(4, 400, 128),) * 4,
        in_specs=vmem(2),
        out_specs=tuple(vmem(5)),
        compiler_params=params(),
        name="assemble",
    )(got, bias_out)
    after, before = along(own, -1), along(own, 1)
    for d in range(1, 4):
        pays[d] = lax.ppermute(pays[d], ("xh", "yl"), [(n, n ^ FLIPS[d]) for n in range(4)])
    k_far, v_far = along(before[:, :128], 1), along(after[:, 128:256], -1)
    *dq_parts, own, up, dk_far, dv_far, down, db_parts = pl.pallas_call(
        functools.partial(attend_kernel, scale),
        out_shape=(shape(4, 128, 128),) * 4
        + (shape(4, 256, 128),) * 2
        + (shape(4, 128, 128),) * 2
        + (shape(4, 256, 128), shape(16, 128, 128)),
        in_specs=[smem] + vmem(9),
        out_specs=tuple(vmem(10)),
        scratch_shapes=[pltpu.VMEM((512, 512), F32), pltpu.VMEM((512, 512), F32)],
        compiler_params=params(),
        name="attend",
    )(where, *pays, own, after, k_far, v_far, before)
    up_more, down_more = along(dk_far, 1), along(dv_far, -1)
    up, down = pl.pallas_call(
        fold_kernel,
        out_shape=(shape(4, 256, 128),) * 2,
        in_specs=vmem(4),
        out_specs=tuple(vmem(2)),
        compiler_params=params(),
        name="fold",
    )(up, up_more, down, down_more)
    db = lax.all_to_all(db_parts, ("z", "xh"), 0, 0)
    for d in (1,):
        dq_parts[d] = lax.ppermute(dq_parts[d], ("xh", "yl"), [(n, n ^ FLIPS[d]) for n in range(4)])
    up, down, dq_parts = lax.optimization_barrier((up, down, dq_parts))
    for d in (2, 3):
        dq_parts[d] = lax.ppermute(dq_parts[d], ("xh", "yl"), [(n, n ^ FLIPS[d]) for n in range(4)])
    up, down = along(up, 1), along(down, -1)
    db = jnp.sum(db.reshape(8, 2, 128, 128).astype(F32), axis=0)
    db = lax.ppermute(db, ("z", "yl"), swaps())
    joined = pl.pallas_call(
        join_kernel,
        out_shape=shape(4, 512, 128),
        in_specs=vmem(8),
        out_specs=vmem()[0],
        compiler_params=params(),
        name="join",
    )(own, up, down, db, *dq_parts)
    joined = lax.all_to_all(joined, ("xl", "c"), 0, 0)
    query_grad, key_grad, value_grad, bias_grad = pl.pallas_call(
        unpack_kernel,
        out_shape=(shape(4, 128, 128),) * 3 + (jax.ShapeDtypeStruct((4, 64, 128), F32),),
        in_specs=vmem(1),
        out_specs=tuple(vmem(4)),
        compiler_params=params(),
        name="unpack",
    )(joined)
    return query_grad, key_grad, value_grad, bias_grad.transpose(0, 2, 1)


def solution(mesh):
    fine = Mesh(mesh.devices.reshape(2, 8, 2, 2, 4, 2), ROW + BLK)
    rows = P(ROW, BLK, None)
    in_specs = (rows, rows, rows, P(None, BLK, None), rows, rows, P(ROW, None, BLK))
    out_specs = (rows, rows, rows, P(None, BLK, ROW))
    return jax.shard_map(body, mesh=fine, in_specs=in_specs, out_specs=out_specs, check_vma=False)
```
